32 devices in a mesh: branch: 2 (over core), tm: 8 (over z, y), tok: 2 (over x).
Axes of the slice: x: 2, y: 2, z: 4, core: 2. Of those that a mesh axis runs over, the one named last changes fastest.
Arguments:
- states: float32 [8, 128, 3072], P('tm', 'tok'), may hold values from -6 to 6
- start_state: float32 [128, 3072], P('tok', 'branch'), may hold values from -12 to 12
- timesteps: int32 [8], P('tm'), may hold values from 0 to 49
- guidance_index: int32 [1], replicated, may hold values from 0 to 7
- modulation: float32 [2, 3, 3072], P('branch'), may hold values from -2.5 to 2.5
- w_query: bfloat16 [3072, 2048], P('branch', 'tok'), may hold values from -6 to 6, as said below
- w_key: bfloat16 [3072, 2048], P('branch', 'tok'), may hold values from -6 to 6, as said below
- w_value: bfloat16 [3072, 2048], P('branch', 'tok'), may hold values from -0.109375 to 0.109375
- w_out: bfloat16 [2048, 3072], P('tok', 'branch'), may hold values from -0.5 to 0.5
Outputs:
- updated_states: float32 [8, 128, 3072], P('tm', 'tok', 'branch')
The draws below stay inside these ranges and needn't reach their ends.
Inputs may be any that keep to these rules, and one draw needn't show every extreme that they name: `w_query`: independent entries of mean zero. `w_key`: independent entries of mean zero.
All inputs are finite; a program needn't handle non-finite values.
Results may differ from the reference program's by a relative error of at most 0.0085.
The reference program's roundings to bfloat16 on the way count: a program that leaves them out, or rounds other values in their place, can miss the bound.
Values may be sent and summed in bfloat16 or wider, within the bound.
No kernel may reach another device: no remote copies, remote signals or barrier semaphores. Data moves between devices by JAX's collectives and lax.ppermute only.
A program may use at most 64 MiB of HBM per device.

```python
import math
import jax
import jax.numpy as jnp
from jax import lax

D = 3072
HEADS = 16
HD = 128
NSTEPS = 50
LAT = 128
W = 8
N_TOK = 2


def projection_draw(seed_key):
    values = jnp.clip(jax.random.normal(seed_key, (D, HEADS * HD), jnp.float32), -6.0, 6.0) * D ** (-0.5)
    return values.astype(jnp.bfloat16)


def draw_w_query(key, part):
    return projection_draw(jax.random.fold_in(key, 11))


def draw_w_key(key, part):
    return projection_draw(jax.random.fold_in(key, 23))


def plant(values, rng, least, largest):
    shape = values.shape
    place = [jax.random.randint(jax.random.fold_in(rng, axis), (), 0, shape[axis]) for axis in range(len(shape))]
    values = values.at[tuple(place)].set(least)
    longest = shape.index(max(shape))
    place[longest] = (place[longest] + 1) % shape[longest]
    return values.at[tuple(place)].set(largest)


def steps_of(own_key, dims, cuts, least, largest):
    def one(axis_at, shards_of):
        draws = jax.random.uniform(jax.random.fold_in(jax.random.fold_in(own_key, 6), axis_at), (shards_of,), jnp.float32, least / len(cuts), largest / len(cuts))
        return jnp.repeat(jnp.exp(draws), dims[axis_at] // shards_of).reshape((-1,) + (1,) * (len(dims) - axis_at - 1))

    level = one(*cuts[0])
    for cut in cuts[1:]:
        level = level * one(*cut)
    return level


def centred(own_key, shape, deviation, bound, pieces=(), kind=jnp.bfloat16):
    array = jax.random.normal(own_key, shape, jnp.float32) * deviation
    if len(pieces) > 0:
        array = steps_of(own_key, shape, pieces, -0.22, 0.18) * array
    return jnp.clip(array, min=-bound, max=bound).astype(kind)


def setup_inputs(seed: int = 0) -> dict:
    seeds = jax.random.split(jax.random.key(seed), 10)
    return {
        "states": centred(seeds[0], (W, LAT, D), 1.0, 6.0, ((0, 8), (1, 2)), jnp.float32),
        "start_state": centred(seeds[1], (LAT, D), 2.0, 12.0, ((0, 2), (1, 2)), jnp.float32),
        "timesteps": plant(jax.random.randint(seeds[2], (W,), 0, NSTEPS), jax.random.fold_in(seeds[2], 1), 0, NSTEPS - 1).astype(jnp.int32),
        "guidance_index": jax.random.randint(seeds[3], (1,), 0, 8).astype(jnp.int32),
        "modulation": centred(seeds[4], (2, 3, D), 0.5, 2.5, ((0, 2),), jnp.float32),
        "w_query": draw_w_query(jax.random.fold_in(seeds[9], 71), 0),
        "w_key": draw_w_key(jax.random.fold_in(seeds[9], 71), 0),
        "w_value": centred(seeds[7], (D, HEADS * HD), D ** -0.5, 0.109375, ((0, 2), (1, 2))),
        "w_out": centred(seeds[8], (HEADS * HD, D), (HEADS * HD // 16) ** -0.5, 0.5, ((0, 2), (1, 2))),
    }


def embed(step_ids, model_width):
    half_width = model_width // 2
    frequency = jnp.exp(-math.log(10000.0) * jnp.arange(half_width, dtype=jnp.float32) / half_width)
    phases = step_ids.astype(jnp.float32)[:, None] * frequency[None, :]
    return jnp.concatenate([jnp.sin(phases), jnp.cos(phases)], axis=1)

def branch_drift(state_now, embedding, modulation_row, w_query, w_key, w_value, w_out):
    mean_value = lax.optimization_barrier(jnp.mean(state_now, axis=1, keepdims=True))
    centered = state_now - mean_value
    variance = lax.optimization_barrier(jnp.mean(centered * centered, axis=1, keepdims=True))
    normed = centered / jnp.sqrt(variance + 1e-06)
    modulated = (normed * (1.0 + modulation_row[1]) + modulation_row[0] + embedding).astype(jnp.bfloat16)
    query_proj = jnp.dot(modulated, w_query, preferred_element_type=jnp.float32).astype(jnp.bfloat16)
    key_proj = jnp.dot(modulated, w_key, preferred_element_type=jnp.float32).astype(jnp.bfloat16)
    value_proj = jnp.dot(modulated, w_value, preferred_element_type=jnp.float32).astype(jnp.bfloat16)
    query_heads = query_proj.reshape(LAT, HEADS, HD).astype(jnp.float32)
    key_heads = key_proj.reshape(LAT, HEADS, HD).astype(jnp.float32)
    value_heads = value_proj.reshape(LAT, HEADS, HD).astype(jnp.float32)
    scores = jnp.einsum('qhc,khc->hqk', query_heads, key_heads) * (1.0 / math.sqrt(HD))
    softmax_w = jax.nn.softmax(scores, axis=-1).astype(jnp.bfloat16)
    attended = jnp.einsum('hqk,khc->qhc', softmax_w.astype(jnp.float32), value_heads).astype(jnp.bfloat16)
    group_cols = HEADS * HD // N_TOK
    groups = attended.reshape(LAT, N_TOK, group_cols).astype(jnp.float32)
    out_groups = w_out.reshape(N_TOK, group_cols, D).astype(jnp.float32)
    partial_value = jnp.einsum('lgc,gcd->gld', groups, out_groups).astype(jnp.bfloat16)
    partial_value = lax.optimization_barrier(partial_value).astype(jnp.float32)
    projected = lax.optimization_barrier(jnp.sum(partial_value, axis=0))
    return (1.0 + modulation_row[2]) * projected

def reference(states, start_state, timesteps, guidance_index, modulation, w_query, w_key, w_value, w_out):
    guide_scale = 1.5 + 0.5 * guidance_index[0].astype(jnp.float32)

    def per_point(pair):
        state_now, step_id = pair
        embedding = embed(step_id[None], D)[0]
        conditional = branch_drift(state_now, embedding, modulation[0], w_query, w_key, w_value, w_out)
        unconditional = branch_drift(state_now, embedding, modulation[1], w_query, w_key, w_value, w_out)
        return unconditional + guide_scale * (conditional - unconditional)
    guided = lax.map(per_point, (states, timesteps))
    step_size = 2.0 * (1.0 + timesteps.astype(jnp.float32)) / NSTEPS
    increment = step_size[:, None, None] * guided
    return start_state[None, :, :] + jnp.cumsum(increment, axis=0)
```

```python
import functools
import math

import jax
import jax.numpy as jnp
from jax import lax
from jax.experimental import pallas as pl
from jax.experimental.pallas import tpu as pltpu
from jax.sharding import PartitionSpec as P

HD = 128
NSTEPS = 50
F32 = jnp.float32
BF16 = jnp.bfloat16
VMEM = pl.BlockSpec(memory_space=pltpu.VMEM)
SMEM = pl.BlockSpec(memory_space=pltpu.SMEM)


def xor_permute(x, axes, mask):
    return lax.ppermute(x, axes, [(i, i ^ mask) for i in range(lax.axis_size(axes))])


def dot(a, b):
    return jnp.dot(a, b, preferred_element_type=F32)


def embed_half(step_id, half_width, branch_index):
    frequency = jnp.exp(-math.log(10000.0) * jnp.arange(half_width, dtype=F32) / half_width)
    phases = step_id.astype(F32) * frequency
    return jnp.where(branch_index == 0, jnp.sin(phases), jnp.cos(phases))[None, :]


def norm_kernel(branch_ref, states_ref, out_ref):
    half_width = out_ref.shape[1]
    tokens = states_ref[...]
    width = tokens.shape[1]
    mean = jnp.sum(tokens, axis=1, keepdims=True) * (1.0 / width)
    centered = tokens - mean
    variance = jnp.sum(centered * centered, axis=1, keepdims=True) * (1.0 / width)
    deviation = jnp.sqrt(variance + 1e-06)
    start = pl.multiple_of(branch_ref[0] * half_width, HD)
    out_ref[...] = (states_ref[:, pl.ds(start, half_width)] - mean) / deviation


def normed_half(states, branch_index):
    rows, width = states.shape
    return pl.pallas_call(
        norm_kernel,
        out_shape=jax.ShapeDtypeStruct((rows, width // 2), F32),
        in_specs=[SMEM, VMEM],
        out_specs=VMEM,
    )(branch_index[None], states)


def attention_kernel(blocks, *refs):
    out_ref = refs[-1]
    rows = refs[0].shape[0]
    columns = refs[0].shape[1]

    def part(which, head):
        sl = slice(head * HD, (head + 1) * HD)
        pieces = []
        for block in range(blocks):
            mine, other = refs[(block * 3 + which) * 2], refs[(block * 3 + which) * 2 + 1]
            pieces.append((mine[0:rows // 2, sl] + other[:, sl]).astype(BF16))
        return jnp.concatenate(pieces, axis=0)

    for head in range(columns // HD):
        query, key, value = part(0, head), part(1, head), part(2, head)
        scores = lax.dot_general(query, key, (((1,), (1,)), ((), ())), preferred_element_type=F32)
        scores = scores * (1.0 / math.sqrt(HD))
        scores = jnp.exp(scores - jnp.max(scores, axis=1, keepdims=True))
        probs = (scores / jnp.sum(scores, axis=1, keepdims=True)).astype(BF16)
        out_ref[:, head * HD:(head + 1) * HD] = dot(probs, value).astype(BF16)


def attention(blocks):
    flat = [array for block in blocks for pair in block for array in pair]
    rows, columns = blocks[0][0][1].shape
    return pl.pallas_call(
        functools.partial(attention_kernel, len(blocks)),
        out_shape=jax.ShapeDtypeStruct((rows * len(blocks), columns), BF16),
        in_specs=[VMEM] * len(flat),
        out_specs=VMEM,
        compiler_params=pltpu.CompilerParams(vmem_limit_bytes=32 << 20),
    )(*flat)


def project_kernel(chunk, ints_ref, floats_ref, mine_ref, other_ref, w_ref, gates_ref, out_ref):
    lat = mine_ref.shape[0]
    columns = w_ref.shape[1]
    both = jnp.concatenate([mine_ref[...], other_ref[...]], axis=0)
    first = ints_ref[0] == 0
    scale, step = floats_ref[0], floats_ref[1]
    for start in range(0, columns, chunk):
        sl = slice(start, start + chunk)
        partial = dot(both, w_ref[:, sl]).astype(BF16).astype(F32)
        mine = (1.0 + gates_ref[0:1, sl]) * partial[:lat]
        other = (1.0 + gates_ref[1:2, sl]) * partial[lat:]
        conditional = jnp.where(first, mine, other)
        unconditional = jnp.where(first, other, mine)
        out_ref[:, sl] = step * (unconditional + scale * (conditional - unconditional))


def project(branch_index, scale, step, mine, other, w_out, gates):
    lat = mine.shape[0]
    columns = w_out.shape[1]
    chunk = 512 if columns % 512 == 0 else HD
    return pl.pallas_call(
        functools.partial(project_kernel, chunk),
        out_shape=jax.ShapeDtypeStruct((lat, columns), F32),
        in_specs=[SMEM, SMEM, VMEM, VMEM, VMEM, VMEM],
        out_specs=VMEM,
        compiler_params=pltpu.CompilerParams(vmem_limit_bytes=32 << 20),
    )(branch_index[None], jnp.stack([scale, step]), mine, other, w_out, gates)


def scan_general(parts):
    total = parts[0]
    for mask in range(1, len(parts)):
        total = total + xor_permute(parts[mask].astype(BF16), "tok", mask).astype(F32)
    position = lax.axis_index("tm")
    result, group = total, total
    mask = 1
    while mask < lax.axis_size("tm"):
        received = xor_permute(group.astype(BF16), "tm", mask).astype(F32)
        result = result + jnp.where(position & mask != 0, received, 0.0)
        group = group + received
        mask *= 2
    return result


def scan_planes(parts):
    axes = ("tm", "tok")
    position = lax.axis_index("tm")
    odd = position & 1 == 1
    rows = parts[0].shape[0] // 2

    def near(x):
        return jnp.where(odd, x[rows:], x[:rows])

    def far(x):
        return jnp.where(odd, x[:rows], x[rows:])

    diagonal = xor_permute(far(parts[1]).astype(BF16), axes, 3)
    across = xor_permute(near(parts[1]).astype(BF16), axes, 1)
    beside = xor_permute(far(parts[0]).astype(BF16), axes, 2)
    own_time = near(parts[0]) + across.astype(F32)
    pair_time = beside.astype(F32) + diagonal.astype(F32)
    group = own_time + pair_time
    earlier = jnp.zeros_like(group)
    mask = 2
    while mask < lax.axis_size("tm"):
        received = xor_permute(group.astype(BF16), "tm", mask).astype(F32)
        earlier = earlier + jnp.where(position & mask != 0, received, 0.0)
        group = group + received
        mask *= 2
    own = earlier + own_time + jnp.where(odd, pair_time, 0.0)
    for_pair = earlier + pair_time + jnp.where(odd, 0.0, own_time)
    returned = xor_permute(for_pair.astype(BF16), "tm", 1).astype(F32)
    return jnp.concatenate([jnp.where(odd, returned, own), jnp.where(odd, own, returned)], axis=0)


def body(
    states, start_state, timesteps, guidance_index, modulation, w_query, w_key, w_value, w_out
):
    tok_count = lax.axis_size("tok")
    branch_index = lax.axis_index("branch")
    rows, model_width = states.shape[1:]
    half_width = model_width // 2
    own_modulation = modulation[0]
    half = functools.partial(
        lax.dynamic_slice_in_dim, start_index=branch_index * half_width, slice_size=half_width, axis=1
    )
    other_modulation = xor_permute(own_modulation, "branch", 1)
    mods = [half(own_modulation), half(other_modulation)]
    embedding = embed_half(timesteps[0], half_width, branch_index)

    normed = normed_half(states[0], branch_index)
    tokens = [normed] + [xor_permute(normed, "tok", mask) for mask in range(1, tok_count)]

    blocks = []
    for block in tokens:
        modulated = jnp.concatenate(
            [block * (1.0 + mod[1:2]) + mod[0:1] + embedding for mod in mods], axis=0
        ).astype(BF16)
        projected = [dot(modulated, w) for w in (w_query, w_key, w_value)]
        blocks.append([(p, xor_permute(p[rows:], "branch", 1)) for p in projected])
    attended = attention(blocks)
    attended_other = xor_permute(attended, "branch", 1)

    guide_scale = 1.5 + 0.5 * guidance_index[0].astype(F32)
    step_size = 2.0 * (1.0 + timesteps[0].astype(F32)) / NSTEPS
    gates = jnp.concatenate([mods[0][2:3], mods[1][2:3]], axis=0)
    increments = project(
        branch_index, guide_scale, step_size, attended, attended_other, w_out, gates
    )
    parts = [increments[m * rows:(m + 1) * rows] for m in range(tok_count)]
    pairs = tok_count == 2 and lax.axis_size("tm") % 2 == 0 and rows % 32 == 0
    scan = scan_planes if pairs else scan_general
    return (start_state + scan(parts))[None]


def solution(mesh):
    in_specs = (
        P("tm", "tok", None),
        P("tok", "branch"),
        P("tm"),
        P(),
        P("branch", None, None),
        P("branch", "tok"),
        P("branch", "tok"),
        P("branch", "tok"),
        P("tok", "branch"),
    )
    out_specs = P("tm", "tok", "branch")
    return jax.shard_map(body, mesh=mesh, in_specs=in_specs, out_specs=out_specs, check_vma=False)
```

```python
import functools
import math

import jax
import jax.numpy as jnp
from jax import lax
from jax.experimental import pallas as pl
from jax.experimental.pallas import tpu as pltpu
from jax.sharding import PartitionSpec as P

HD = 128
NSTEPS = 50
F32 = jnp.float32
BF16 = jnp.bfloat16
VMEM = pl.BlockSpec(memory_space=pltpu.VMEM)
SMEM = pl.BlockSpec(memory_space=pltpu.SMEM)
HBM = pl.BlockSpec(memory_space=pltpu.HBM)


def xor_permute(x, axes, mask):
    return lax.ppermute(x, axes, [(i, i ^ mask) for i in range(lax.axis_size(axes))])


def dot(a, b):
    return jnp.dot(a, b, preferred_element_type=F32)


def embed_half(step_id, half_width, branch_index):
    frequency = jnp.exp(-math.log(10000.0) * jnp.arange(half_width, dtype=F32) / half_width)
    phases = step_id.astype(F32) * frequency
    return jnp.where(branch_index == 0, jnp.sin(phases), jnp.cos(phases))[None, :]


def in_vmem(*arrays):
    return [pltpu.with_memory_space_constraint(array, pltpu.VMEM) for array in arrays]


def in_hbm(*arrays):
    return [pltpu.with_memory_space_constraint(array, pltpu.HBM) for array in arrays]


def call(kernel, out_shape, in_specs, out_specs, scratch_shapes=()):
    return pl.pallas_call(
        kernel,
        out_shape=out_shape,
        in_specs=in_specs,
        out_specs=out_specs,
        scratch_shapes=scratch_shapes,
        compiler_params=pltpu.CompilerParams(vmem_limit_bytes=16 << 20),
    )


def norm_kernel(pieces, branch_ref, states_ref, out_ref, tokens_ref, sems):
    half_width = out_ref.shape[1]
    rows, width = tokens_ref.shape
    size = rows // pieces
    copies = []
    for piece in range(pieces):
        sl = slice(piece * size, (piece + 1) * size)
        copy = pltpu.make_async_copy(states_ref.at[sl], tokens_ref.at[sl], sems.at[piece])
        copy.start()
        copies.append(copy)
    start = pl.multiple_of(branch_ref[0] * half_width, HD)
    for piece in range(pieces):
        sl = slice(piece * size, (piece + 1) * size)
        copies[piece].wait()
        tokens = tokens_ref[sl, :]
        mean = jnp.sum(tokens, axis=1, keepdims=True) * (1.0 / width)
        centered = tokens - mean
        variance = jnp.sum(centered * centered, axis=1, keepdims=True) * (1.0 / width)
        inverse = 1.0 / jnp.sqrt(variance + 1e-06)
        out_ref[sl, :] = (tokens_ref[sl, pl.ds(start, half_width)] - mean) * inverse


def normed_half(states, branch_index):
    rows, width = states.shape
    pieces = 4
    return call(
        functools.partial(norm_kernel, pieces),
        pltpu.VMEM((rows, width // 2), F32),
        [SMEM, HBM],
        VMEM,
        [pltpu.VMEM((rows, width), F32), pltpu.SemaphoreType.DMA((pieces,))],
    )(branch_index[None], *in_hbm(states))


def halves_kernel(branch_ref, modulation_ref, mine_ref, send_ref):
    half_width = mine_ref.shape[2]
    branch = branch_ref[0]
    for row in range(mine_ref.shape[0]):
        mine_ref[row] = modulation_ref[row, :, pl.ds(pl.multiple_of(branch * half_width, HD), half_width)]
        send_ref[row] = modulation_ref[
            row, :, pl.ds(pl.multiple_of((1 - branch) * half_width, HD), half_width)
        ]


def modulation_halves(modulation, branch_index):
    rows, _, width = modulation.shape
    out = pltpu.VMEM((rows, 1, width // 2), F32)
    return call(halves_kernel, [out, out], [SMEM, VMEM], [VMEM, VMEM])(branch_index[None], modulation)


def modulate_and_project(tokens_ref, mine_ref, other_ref, embedding_ref, weights, keep_ref, send_ref):
    rows = tokens_ref.shape[0]
    tokens = tokens_ref[...]
    embedding = embedding_ref[...]
    modulated = jnp.concatenate(
        [
            (tokens * (1.0 + mod_ref[1]) + mod_ref[0] + embedding).astype(BF16)
            for mod_ref in (mine_ref, other_ref)
        ],
        axis=0,
    )
    column = 0
    for weight_ref, ready in weights:
        ready()
        columns = weight_ref.shape[1]
        chunk = min(columns, 512)
        for start in range(0, columns, chunk):
            projected = dot(modulated, weight_ref[:, start:start + chunk])
            sl = slice(column + start, column + start + chunk)
            keep_ref[:, sl] = projected[:rows]
            send_ref[:, sl] = projected[rows:]
        column += columns


def first_kernel(*refs):
    tokens_ref, mine_ref, other_ref, embedding_ref = refs[:4]
    sources, targets = refs[4:8], refs[8:12]
    keep_ref, send_ref, sems = refs[12:]
    copies = [
        pltpu.make_async_copy(source, target, sems.at[i])
        for i, (source, target) in enumerate(zip(sources, targets))
    ]
    for copy in copies:
        copy.start()
    weights = [(target, copy.wait) for target, copy in zip(targets[:3], copies[:3])]
    modulate_and_project(tokens_ref, mine_ref, other_ref, embedding_ref, weights, keep_ref, send_ref)
    copies[3].wait()


def project_first(tokens, mine, other, embedding, weights):
    out = pltpu.VMEM((tokens.shape[0], 3 * weights[0].shape[1]), F32)
    result = call(
        first_kernel,
        [pltpu.VMEM(w.shape, w.dtype) for w in weights] + [out, out],
        [VMEM] * 4 + [HBM] * 4,
        [VMEM] * 6,
        [pltpu.SemaphoreType.DMA((4,))],
    )(*in_vmem(tokens, mine, other, embedding), *in_hbm(*weights))
    return result[:4], result[4], result[5]


def later_kernel(tokens_ref, mine_ref, other_ref, embedding_ref, wq_ref, wk_ref, wv_ref, keep_ref, send_ref):
    weights = [(ref, lambda: None) for ref in (wq_ref, wk_ref, wv_ref)]
    modulate_and_project(tokens_ref, mine_ref, other_ref, embedding_ref, weights, keep_ref, send_ref)


def project_later(tokens, mine, other, embedding, weights):
    out = pltpu.VMEM((tokens.shape[0], 3 * weights[0].shape[1]), F32)
    return call(later_kernel, [out, out], [VMEM] * 7, [VMEM] * 2)(
        *in_vmem(tokens, mine, other, embedding, *weights)
    )


def attention_kernel(*refs):
    out_ref = refs[-1]
    blocks = [(refs[i], refs[i + 1]) for i in range(0, len(refs) - 1, 2)]
    columns = out_ref.shape[1]

    def part(which, head):
        sl = slice(which * columns + head * HD, which * columns + (head + 1) * HD)
        return jnp.concatenate(
            [(mine[:, sl] + other[:, sl]).astype(BF16) for mine, other in blocks], axis=0
        )

    heads = columns // HD
    all_scores = [
        lax.dot_general(
            part(0, head), part(1, head), (((1,), (1,)), ((), ())), preferred_element_type=F32
        )
        for head in range(heads)
    ]
    all_probs = []
    for scores in all_scores:
        scores = scores * (1.0 / math.sqrt(HD))
        scores = jnp.exp(scores - jnp.max(scores, axis=1, keepdims=True))
        all_probs.append((scores / jnp.sum(scores, axis=1, keepdims=True)).astype(BF16))
    for head, probs in enumerate(all_probs):
        out_ref[:, head * HD:(head + 1) * HD] = dot(probs, part(2, head)).astype(BF16)


def attention(blocks):
    flat = [array for block in blocks for array in block]
    rows, columns = flat[0].shape
    return call(
        attention_kernel,
        pltpu.VMEM((rows * len(blocks), columns // 3), BF16),
        [VMEM] * len(flat),
        VMEM,
    )(*in_vmem(*flat))


def project_kernel(floats_ref, mine_ref, other_ref, w_ref, mine_mod_ref, other_mod_ref, *out_refs):
    lat = mine_ref.shape[0]
    rows, columns = out_refs[0].shape
    both = jnp.concatenate([mine_ref[...], other_ref[...]], axis=0)
    mine_factor, other_factor = floats_ref[0], floats_ref[1]
    chunk = 512 if columns % 512 == 0 else HD
    for start in range(0, columns, chunk):
        sl = slice(start, start + chunk)
        partial = dot(both, w_ref[:, sl]).astype(BF16).astype(F32)
        mine = mine_factor * (1.0 + mine_mod_ref[2, :, sl])
        other = other_factor * (1.0 + other_mod_ref[2, :, sl])
        for block, out_ref in enumerate(out_refs):
            here = block * rows
            out_ref[:, sl] = (
                mine * partial[here:here + rows] + other * partial[lat + here:lat + here + rows]
            )


def project(factors, mine, other, w_out, mine_mod, other_mod, blocks):
    lat = mine.shape[0]
    columns = w_out.shape[1]
    return call(
        project_kernel,
        [pltpu.VMEM((lat // blocks, columns), F32)] * blocks,
        [SMEM] + [VMEM] * 5,
        [VMEM] * blocks,
    )(factors, *in_vmem(mine, other, w_out, mine_mod, other_mod))


def scan_general(parts):
    total = parts[0]
    for mask in range(1, len(parts)):
        total = total + xor_permute(parts[mask].astype(BF16), "tok", mask).astype(F32)
    position = lax.axis_index("tm")
    result, group = total, total
    mask = 1
    while mask < lax.axis_size("tm"):
        received = xor_permute(group.astype(BF16), "tm", mask).astype(F32)
        result = result + jnp.where(position & mask != 0, received, 0.0)
        group = group + received
        mask *= 2
    return result


def scan_planes(parts):
    axes = ("tm", "tok")
    position = lax.axis_index("tm")
    odd = position & 1 == 1
    rows = parts[0].shape[0] // 2

    def near(x):
        return jnp.where(odd, x[rows:], x[:rows])

    def far(x):
        return jnp.where(odd, x[:rows], x[rows:])

    diagonal = xor_permute(far(parts[1]).astype(BF16), axes, 3)
    across = xor_permute(near(parts[1]).astype(BF16), axes, 1)
    beside = xor_permute(far(parts[0]).astype(BF16), axes, 2)
    own_time = near(parts[0]) + across.astype(F32)
    pair_time = beside.astype(F32) + diagonal.astype(F32)
    group = own_time + pair_time
    earlier = jnp.zeros_like(group)
    mask = 2
    while mask < lax.axis_size("tm"):
        received = xor_permute(group.astype(BF16), "tm", mask).astype(F32)
        earlier = earlier + jnp.where(position & mask != 0, received, 0.0)
        group = group + received
        mask *= 2
    own = earlier + own_time + jnp.where(odd, pair_time, 0.0)
    for_pair = earlier + pair_time + jnp.where(odd, 0.0, own_time)
    returned = xor_permute(for_pair.astype(BF16), "tm", 1).astype(F32)
    return jnp.concatenate([jnp.where(odd, returned, own), jnp.where(odd, own, returned)], axis=0)


def body(
    states, start_state, timesteps, guidance_index, modulation, w_query, w_key, w_value, w_out
):
    tok_count = lax.axis_size("tok")
    branch_index = lax.axis_index("branch")
    rows, model_width = states.shape[1:]
    half_width = model_width // 2
    normed = normed_half(states[0], branch_index)
    tokens = [normed] + [xor_permute(normed, "tok", mask) for mask in range(1, tok_count)]

    mine_mod, send_mod = modulation_halves(jnp.transpose(modulation, (1, 0, 2)), branch_index)
    other_mod = xor_permute(send_mod, "branch", 1)
    embedding = embed_half(timesteps[0], half_width, branch_index)

    weights, keep, send = project_first(
        tokens[0], mine_mod, other_mod, embedding, (w_query, w_key, w_value, w_out)
    )
    blocks = [(keep, xor_permute(send, "branch", 1))]
    for block in tokens[1:]:
        keep, send = project_later(block, mine_mod, other_mod, embedding, weights[:3])
        blocks.append((keep, xor_permute(send, "branch", 1)))
    attended = attention(blocks)
    attended_other = xor_permute(attended, "branch", 1)

    guide_scale = 1.5 + 0.5 * guidance_index[0].astype(F32)
    step_size = 2.0 * (1.0 + timesteps[0].astype(F32)) / NSTEPS
    factors = step_size * jnp.stack([guide_scale, 1.0 - guide_scale])
    factors = jnp.where(branch_index == 0, factors, factors[::-1])
    parts = project(factors, attended, attended_other, weights[3], mine_mod, other_mod, tok_count)
    pairs = tok_count == 2 and lax.axis_size("tm") % 2 == 0 and rows % 32 == 0
    scan = scan_planes if pairs else scan_general
    return (start_state + scan(parts))[None]


def solution(mesh):
    in_specs = (
        P("tm", "tok", None),
        P("tok", "branch"),
        P("tm"),
        P(),
        P("branch", None, None),
        P("branch", "tok"),
        P("branch", "tok"),
        P("branch", "tok"),
        P("tok", "branch"),
    )
    out_specs = P("tm", "tok", "branch")
    return jax.shard_map(body, mesh=mesh, in_specs=in_specs, out_specs=out_specs, check_vma=False)
```

```python
import functools
import math

import jax
import jax.numpy as jnp
from jax import lax
from jax.experimental import pallas as pl
from jax.experimental.pallas import tpu as pltpu
from jax.sharding import PartitionSpec as P

HD = 128
NSTEPS = 50
F32 = jnp.float32
BF16 = jnp.bfloat16
VMEM = pl.BlockSpec(memory_space=pltpu.VMEM)
SMEM = pl.BlockSpec(memory_space=pltpu.SMEM)
ANY = pl.BlockSpec(memory_space=pl.ANY)
HBM = pl.BlockSpec(memory_space=pltpu.HBM)


def xor_permute(x, axes, mask):
    return lax.ppermute(x, axes, [(i, i ^ mask) for i in range(lax.axis_size(axes))])


def dot(a, b):
    return jnp.dot(a, b, preferred_element_type=F32)


def embed_half(step_ids, half_width, branch_index):
    frequency = jnp.exp(-math.log(10000.0) * jnp.arange(half_width, dtype=F32) / half_width)
    phases = step_ids.astype(F32)[:, None] * frequency[None, :]
    return jnp.where(branch_index == 0, jnp.sin(phases), jnp.cos(phases))


def in_vmem(*arrays):
    return [pltpu.with_memory_space_constraint(array, pltpu.VMEM) for array in arrays]


def in_hbm(*arrays):
    return [pltpu.with_memory_space_constraint(array, pltpu.HBM) for array in arrays]


def call(kernel, out_shape, in_specs, out_specs, scratch_shapes=()):
    return pl.pallas_call(
        kernel,
        out_shape=out_shape,
        in_specs=in_specs,
        out_specs=out_specs,
        scratch_shapes=scratch_shapes,
        compiler_params=pltpu.CompilerParams(vmem_limit_bytes=6 << 20),
    )


def norm_kernel(pieces, branch_ref, states_ref, *refs):
    out_refs, (tokens_ref, sems) = refs[:-2], refs[-2:]
    width = out_refs[0].shape[1]
    rows, model_width = tokens_ref.shape
    size = rows // pieces
    copies = []
    for piece in range(pieces):
        sl = slice(piece * size, (piece + 1) * size)
        copy = pltpu.make_async_copy(states_ref.at[sl], tokens_ref.at[sl], sems.at[piece])
        copy.start()
        copies.append(copy)
    for piece in range(pieces):
        sl = slice(piece * size, (piece + 1) * size)
        copies[piece].wait()
        tokens = tokens_ref[sl, :]
        mean = jnp.sum(tokens, axis=1, keepdims=True) * (1.0 / model_width)
        centered = tokens - mean
        variance = jnp.sum(centered * centered, axis=1, keepdims=True) * (1.0 / model_width)
        inverse = 1.0 / jnp.sqrt(variance + 1e-06)
        for index, out_ref in enumerate(out_refs):
            start = branch_ref[0] * (model_width // 2) + index * width
            columns = pl.ds(pl.multiple_of(start, HD), width)
            out_ref[sl, :] = (tokens_ref[sl, columns] - mean) * inverse


def normed_half(states, branch_index, cuts):
    rows, width = states.shape
    pieces = 1
    return call(
        functools.partial(norm_kernel, pieces),
        [pltpu.VMEM((rows, width // 2 // cuts), F32)] * cuts,
        [SMEM, HBM],
        [VMEM] * cuts,
        [pltpu.VMEM((rows, width), F32), pltpu.SemaphoreType.DMA((pieces,))],
    )(branch_index[None], *in_hbm(states))


def copy_kernel(source_ref, _, target_ref, sem):
    copy = pltpu.make_async_copy(source_ref, target_ref, sem)
    copy.start()
    copy.wait()


def into_vmem(array, after):
    return call(
        copy_kernel, pltpu.VMEM(array.shape, array.dtype), [HBM, ANY], VMEM, [pltpu.SemaphoreType.DMA]
    )(*in_hbm(array), after)


def modulate(tokens, factors):
    return jnp.concatenate(
        [
            (tokens * factors[i:i + 1] + factors[i + 1:i + 2]).astype(BF16)
            for i in (0, 2)
        ],
        axis=0,
    )


def first_kernel(cuts, branch_ref, step_ref, guidance_ref, *refs):
    tokens_refs, refs = refs[:cuts], refs[cuts:]
    mine_ref, other_ref, embedding_ref, *sources = refs[:6]
    factor_refs, refs = refs[6:6 + cuts], refs[6 + cuts:]
    mine_gate_ref, other_gate_ref, keep_ref, send_ref = refs[:4]
    targets, sems = refs[4:-1], refs[-1]
    width = tokens_refs[0].shape[1]
    copies = []
    for i, source in enumerate(sources):
        for cut in range(cuts):
            copies.append(
                pltpu.make_async_copy(
                    source.at[pl.ds(cut * width, width)], targets[i * cuts + cut], sems.at[i * cuts + cut]
                )
            )
    for copy in copies:
        copy.start()

    first = branch_ref[0] == 0
    step = 2.0 * (1.0 + step_ref[0].astype(F32)) / NSTEPS
    scale = 1.5 + 0.5 * guidance_ref[0].astype(F32)
    conditional, unconditional = step * scale, step * (1.0 - scale)
    base = branch_ref[0] * (width * cuts)
    half = pl.ds(pl.multiple_of(base, HD), width * cuts)
    mine_gate_ref[...] = jnp.where(first, conditional, unconditional) * (1.0 + mine_ref[2, :, half])
    other_gate_ref[...] = jnp.where(first, unconditional, conditional) * (1.0 + other_ref[2, :, half])
    modulated = []
    for cut in range(cuts):
        columns = pl.ds(pl.multiple_of(base + cut * width, HD), width)
        embedding = embedding_ref[:, cut * width:(cut + 1) * width]
        rows = []
        for mod_ref in (mine_ref, other_ref):
            rows += [1.0 + mod_ref[1, :, columns], mod_ref[0, :, columns] + embedding]
        for i, row in enumerate(rows):
            factor_refs[cut][i:i + 1, :] = row
        modulated.append(modulate(tokens_refs[cut][...], rows_of(rows)))
    kept = keep_ref.shape[0]
    for i in range(len(sources)):
        columns = sources[i].shape[1]
        chunk = min(columns, 512)
        for cut in range(cuts):
            copies[i * cuts + cut].wait()
        for start in range(0, columns, chunk):
            projected = sum(
                dot(modulated[cut], targets[i * cuts + cut][:, start:start + chunk]) for cut in range(cuts)
            )
            sl = slice(i * columns + start, i * columns + start + chunk)
            keep_ref[:, sl] = projected[:kept]
            send_ref[:, sl] = projected[kept:]


def rows_of(rows):
    return jnp.concatenate(rows, axis=0)


def project_first(scalars, tokens, mine, other, embedding, weights):
    cuts = len(tokens)
    rows, width = tokens[0].shape
    columns = weights[0].shape[1]
    out = pltpu.VMEM((rows, 3 * columns), F32)
    gate = pltpu.VMEM((1, width * cuts), F32)
    result = call(
        functools.partial(first_kernel, cuts),
        [pltpu.VMEM((4, width), F32)] * cuts
        + [gate, gate, out, out]
        + [pltpu.VMEM((width, columns), BF16)] * (3 * cuts),
        [SMEM] * 3 + [VMEM] * (cuts + 3) + [HBM] * 3,
        [VMEM] * (4 * cuts + 4),
        [pltpu.SemaphoreType.DMA((3 * cuts,))],
    )(*scalars, *tokens, mine, other, embedding, *in_hbm(*weights))
    factors, (mine_gate, other_gate, keep, send), held = result[:cuts], result[cuts:cuts + 4], result[cuts + 4:]
    return factors, mine_gate, other_gate, keep, send, [held[cut::cuts] for cut in range(cuts)]


def later_kernel(added, tokens_ref, factors_ref, wq_ref, wk_ref, wv_ref, *refs):
    refs = list(refs)
    before = [refs.pop(0) for _ in range(2 * added)]
    keep_ref, send_ref = refs
    kept = keep_ref.shape[0]
    modulated = modulate(tokens_ref[...], factors_ref[...])
    for i, weight_ref in enumerate((wq_ref, wk_ref, wv_ref)):
        columns = weight_ref.shape[1]
        chunk = min(columns, 512)
        for start in range(0, columns, chunk):
            projected = dot(modulated, weight_ref[:, start:start + chunk])
            sl = slice(i * columns + start, i * columns + start + chunk)
            keep, send = projected[:kept], projected[kept:]
            if added:
                keep, send = before[0][:, sl] + keep, before[1][:, sl] + send
            keep_ref[:, sl] = keep
            send_ref[:, sl] = send


def project_later(tokens, factors, weights, before=()):
    out = pltpu.VMEM((tokens.shape[0], 3 * weights[0].shape[1]), F32)
    return call(
        functools.partial(later_kernel, len(before) // 2),
        [out, out],
        [VMEM] * (5 + len(before)),
        [VMEM] * 2,
    )(tokens, *in_vmem(factors, *weights, *before))


def attention_kernel(outs, *refs):
    refs, out_refs = refs[:-outs], refs[-outs:]
    blocks = [(refs[i], refs[i + 1]) for i in range(0, len(refs), 2)]
    width = out_refs[0].shape[1]
    columns = width * outs

    def part(which, head):
        sl = slice(which * columns + head * HD, which * columns + (head + 1) * HD)
        return jnp.concatenate(
            [(mine[:, sl] + other[:, sl]).astype(BF16) for mine, other in blocks], axis=0
        )

    heads = columns // HD
    all_scores = [
        lax.dot_general(
            part(0, head), part(1, head), (((1,), (1,)), ((), ())), preferred_element_type=F32
        )
        for head in range(heads)
    ]
    all_probs = []
    for scores in all_scores:
        scores = scores * (1.0 / math.sqrt(HD))
        scores = jnp.exp(scores - jnp.max(scores, axis=1, keepdims=True))
        all_probs.append((scores / jnp.sum(scores, axis=1, keepdims=True)).astype(BF16))
    for head, probs in enumerate(all_probs):
        out, start = divmod(head * HD, width)
        out_refs[out][:, start:start + HD] = dot(probs, part(2, head)).astype(BF16)


def attention(blocks, outs):
    flat = [array for block in blocks for array in block]
    rows, columns = flat[0].shape
    return call(
        functools.partial(attention_kernel, outs),
        [pltpu.VMEM((rows * len(blocks), columns // 3 // outs), BF16)] * outs,
        [VMEM] * len(flat),
        [VMEM] * outs,
    )(*in_vmem(*flat))


def project_kernel(cuts, added, *refs):
    attended_refs, (w_ref, gate_ref, *refs) = refs[:cuts], refs[cuts:]
    out_refs = refs[added:]
    rows, columns = out_refs[0].shape
    chunk = 512 if columns % 512 == 0 else HD
    attended = jnp.concatenate([ref[...] for ref in attended_refs], axis=1)
    for start in range(0, columns, chunk):
        sl = slice(start, start + chunk)
        increment = gate_ref[:, sl] * dot(attended, w_ref[:, sl]).astype(BF16).astype(F32)
        if added:
            increment = refs[0][:, sl] + increment
        for block, out_ref in enumerate(out_refs):
            out_ref[:, sl] = increment[block * rows:(block + 1) * rows]


def project(attended, w_out, gate, before=(), blocks=1):
    return call(
        functools.partial(project_kernel, len(attended), len(before)),
        [pltpu.VMEM((attended[0].shape[0] // blocks, w_out.shape[1]), F32)] * blocks,
        [VMEM] * (2 + len(attended) + len(before)),
        [VMEM] * blocks,
    )(*attended, w_out, *in_vmem(gate, *before))


def scan_general(parts):
    total = parts[0]
    for mask in range(1, len(parts)):
        total = total + xor_permute(parts[mask].astype(BF16), "tok", mask).astype(F32)
    position = lax.axis_index("tm")
    result, group = total, total
    mask = 1
    while mask < lax.axis_size("tm"):
        received = xor_permute(group.astype(BF16), "tm", mask).astype(F32)
        result = result + jnp.where(position & mask != 0, received, 0.0)
        group = group + received
        mask *= 2
    return result


def scan_planes(parts):
    axes = ("tm", "tok")
    position = lax.axis_index("tm")
    odd = position & 1 == 1
    rows = parts[0].shape[0] // 2

    def near(x):
        return jnp.where(odd, x[rows:], x[:rows])

    def far(x):
        return jnp.where(odd, x[:rows], x[rows:])

    diagonal = xor_permute(far(parts[1]).astype(BF16), axes, 3)
    across = xor_permute(near(parts[1]).astype(BF16), axes, 1)
    beside = xor_permute(far(parts[0]).astype(BF16), axes, 2)
    own_time = near(parts[0]) + across.astype(F32)
    pair_time = beside.astype(F32) + diagonal.astype(F32)
    group = own_time + pair_time
    earlier = jnp.zeros_like(group)
    mask = 2
    while mask < lax.axis_size("tm"):
        received = xor_permute(group.astype(BF16), "tm", mask).astype(F32)
        earlier = earlier + jnp.where(position & mask != 0, received, 0.0)
        group = group + received
        mask *= 2
    own = earlier + own_time + jnp.where(odd, pair_time, 0.0)
    for_pair = earlier + pair_time + jnp.where(odd, 0.0, own_time)
    returned = xor_permute(for_pair.astype(BF16), "tm", 1).astype(F32)
    return jnp.concatenate([jnp.where(odd, returned, own), jnp.where(odd, own, returned)], axis=0)


def body(
    states, start_state, timesteps, guidance_index, modulation, w_query, w_key, w_value, w_out
):
    tok_count = lax.axis_size("tok")
    branch_index = lax.axis_index("branch")
    rows, model_width = states.shape[1:]
    half_width = model_width // 2
    cuts = 2
    normed = normed_half(states[0], branch_index, cuts)
    modulation = into_vmem(jnp.transpose(modulation, (1, 0, 2)), normed[0])
    tokens = [
        [xor_permute(piece, "tok", mask) for piece in normed] for mask in range(1, tok_count)
    ]
    other_modulation = xor_permute(modulation, "branch", 1)
    embedding = embed_half(timesteps, half_width, branch_index)

    factors, mine_gate, other_gate, keep, send, weights = project_first(
        (branch_index[None], timesteps, guidance_index),
        normed, modulation, other_modulation, embedding, (w_query, w_key, w_value)
    )
    blocks = [(keep, xor_permute(send, "branch", 1))]
    for block in tokens:
        before = ()
        for cut in range(cuts):
            before = project_later(block[cut], factors[cut], weights[cut], before)
        keep, send = before
        blocks.append((keep, xor_permute(send, "branch", 1)))
    attended = attention(blocks, min(2, w_query.shape[1] // HD))
    attended_other = [xor_permute(array, "branch", 1) for array in attended]
    increments = project(attended, w_out, mine_gate)
    parts = project(attended_other, w_out, other_gate, increments, tok_count)
    pairs = tok_count == 2 and lax.axis_size("tm") % 2 == 0 and rows % 32 == 0
    scan = scan_planes if pairs else scan_general
    return (start_state + scan(parts))[None]


def solution(mesh):
    in_specs = (
        P("tm", "tok", None),
        P("tok", "branch"),
        P("tm"),
        P(),
        P("branch", None, None),
        P("branch", "tok"),
        P("branch", "tok"),
        P("branch", "tok"),
        P("tok", "branch"),
    )
    out_specs = P("tm", "tok", "branch")
    return jax.shard_map(body, mesh=mesh, in_specs=in_specs, out_specs=out_specs, check_vma=False)
```

```python
import functools
import math

import jax
import jax.numpy as jnp
from jax import lax
from jax.experimental import pallas as pl
from jax.experimental.pallas import tpu as pltpu
from jax.sharding import PartitionSpec as P

HD = 128
NSTEPS = 50
F32 = jnp.float32
BF16 = jnp.bfloat16
VMEM = pl.BlockSpec(memory_space=pltpu.VMEM)
SMEM = pl.BlockSpec(memory_space=pltpu.SMEM)
ANY = pl.BlockSpec(memory_space=pl.ANY)
HBM = pl.BlockSpec(memory_space=pltpu.HBM)


def xor_permute(x, axes, mask):
    return lax.ppermute(x, axes, [(i, i ^ mask) for i in range(lax.axis_size(axes))])


def dot(a, b):
    return jnp.dot(a, b, preferred_element_type=F32)


def embed_half(step_ids, half_width, branch_index):
    frequency = jnp.exp(-math.log(10000.0) * jnp.arange(half_width, dtype=F32) / half_width)
    phases = step_ids.astype(F32)[:, None] * frequency[None, :]
    return jnp.where(branch_index == 0, jnp.sin(phases), jnp.cos(phases))


def in_vmem(*arrays):
    return [pltpu.with_memory_space_constraint(array, pltpu.VMEM) for array in arrays]


def in_hbm(*arrays):
    return [pltpu.with_memory_space_constraint(array, pltpu.HBM) for array in arrays]


def call(kernel, out_shape, in_specs, out_specs, scratch_shapes=(), flops=0, moved=0):
    return pl.pallas_call(
        kernel,
        out_shape=out_shape,
        in_specs=in_specs,
        out_specs=out_specs,
        scratch_shapes=scratch_shapes,
        cost_estimate=pl.CostEstimate(flops=flops, bytes_accessed=moved, transcendentals=0),
        compiler_params=pltpu.CompilerParams(vmem_limit_bytes=6 << 20),
    )


def norm_kernel(pieces, branch_ref, states_ref, *refs):
    out_refs, (tokens_ref, sems) = refs[:-2], refs[-2:]
    width = out_refs[0].shape[1]
    rows, model_width = tokens_ref.shape
    size = rows // pieces
    copies = []
    for piece in range(pieces):
        sl = slice(piece * size, (piece + 1) * size)
        copy = pltpu.make_async_copy(states_ref.at[sl], tokens_ref.at[sl], sems.at[piece])
        copy.start()
        copies.append(copy)
    for piece in range(pieces):
        sl = slice(piece * size, (piece + 1) * size)
        copies[piece].wait()
        tokens = tokens_ref[sl, :]
        mean = jnp.sum(tokens, axis=1, keepdims=True) * (1.0 / model_width)
        centered = tokens - mean
        variance = jnp.sum(centered * centered, axis=1, keepdims=True) * (1.0 / model_width)
        inverse = 1.0 / jnp.sqrt(variance + 1e-06)
        for index, out_ref in enumerate(out_refs):
            start = branch_ref[0] * (model_width // 2) + index * width
            columns = pl.ds(pl.multiple_of(start, HD), width)
            out_ref[sl, :] = (tokens_ref[sl, columns] - mean) * inverse


def normed_half(states, branch_index, cuts):
    rows, width = states.shape
    pieces = 1
    return call(
        functools.partial(norm_kernel, pieces),
        [pltpu.VMEM((rows, width // 2 // cuts), F32)] * cuts,
        [SMEM, HBM],
        [VMEM] * cuts,
        [pltpu.VMEM((rows, width), F32), pltpu.SemaphoreType.DMA((pieces,))],
        moved=4 * rows * width,
    )(branch_index[None], *in_hbm(states))


def copy_kernel(source_ref, _, target_ref, sem):
    copy = pltpu.make_async_copy(source_ref, target_ref, sem)
    copy.start()
    copy.wait()


def into_vmem(array, after):
    return call(
        copy_kernel, pltpu.VMEM(array.shape, array.dtype), [HBM, ANY], VMEM, [pltpu.SemaphoreType.DMA],
        moved=4 * array.size,
    )(*in_hbm(array), after)


def modulate(tokens, factors):
    return jnp.concatenate(
        [
            (tokens * factors[i:i + 1] + factors[i + 1:i + 2]).astype(BF16)
            for i in (0, 2)
        ],
        axis=0,
    )


def first_kernel(cuts, groups, branch_ref, step_ref, guidance_ref, *refs):
    tokens_refs, refs = refs[:cuts], refs[cuts:]
    mine_ref, other_ref, embedding_ref, *sources, out_source = refs[:7]
    factor_refs, refs = refs[7:7 + cuts], refs[7 + cuts:]
    mine_gate_ref, other_gate_ref, keep_ref = refs[:3]
    send_refs, targets, (out_target, sems) = refs[3:3 + groups], refs[3 + groups:-2], refs[-2:]
    width = tokens_refs[0].shape[1]
    copies = []
    for i, source in enumerate(sources):
        for cut in range(cuts):
            copies.append(
                pltpu.make_async_copy(
                    source.at[pl.ds(cut * width, width)], targets[i * cuts + cut], sems.at[i * cuts + cut]
                )
            )
    held_rows = out_source.at[pl.ds(0, out_target.shape[0])]
    copies.append(pltpu.make_async_copy(held_rows, out_target, sems.at[len(copies)]))
    for copy in copies:
        copy.start()

    first = branch_ref[0] == 0
    step = 2.0 * (1.0 + step_ref[0].astype(F32)) / NSTEPS
    scale = 1.5 + 0.5 * guidance_ref[0].astype(F32)
    conditional, unconditional = step * scale, step * (1.0 - scale)
    base = branch_ref[0] * (width * cuts)
    half = pl.ds(pl.multiple_of(base, HD), width * cuts)
    mine_gate_ref[...] = jnp.where(first, conditional, unconditional) * (1.0 + mine_ref[2, :, half])
    other_gate_ref[...] = jnp.where(first, unconditional, conditional) * (1.0 + other_ref[2, :, half])
    modulated = []
    for cut in range(cuts):
        columns = pl.ds(pl.multiple_of(base + cut * width, HD), width)
        embedding = embedding_ref[:, cut * width:(cut + 1) * width]
        rows = []
        for mod_ref in (mine_ref, other_ref):
            rows += [1.0 + mod_ref[1, :, columns], mod_ref[0, :, columns] + embedding]
        for i, row in enumerate(rows):
            factor_refs[cut][i:i + 1, :] = row
        modulated.append(modulate(tokens_refs[cut][...], rows_of(rows)))
    kept = keep_ref.shape[0]
    for i in range(len(sources)):
        chunk = sources[i].shape[1] // groups
        for cut in range(cuts):
            copies[i * cuts + cut].wait()
        for group in range(groups):
            columns = slice(group * chunk, (group + 1) * chunk)
            projected = sum(
                dot(modulated[cut], targets[i * cuts + cut][:, columns]) for cut in range(cuts)
            )
            here = (group * 3 + i) * chunk
            keep_ref[:, here:here + chunk] = projected[:kept]
            send_refs[group][:, i * chunk:(i + 1) * chunk] = projected[kept:]
    copies[-1].wait()


def rows_of(rows):
    return jnp.concatenate(rows, axis=0)


def project_first(scalars, tokens, mine, other, embedding, weights, w_out, groups):
    cuts = len(tokens)
    rows, width = tokens[0].shape
    columns = weights[0].shape[1]
    keep = pltpu.VMEM((rows, 3 * columns), F32)
    send = pltpu.VMEM((rows, 3 * columns // groups), F32)
    gate = pltpu.VMEM((1, width * cuts), F32)
    result = call(
        functools.partial(first_kernel, cuts, groups),
        [pltpu.VMEM((4, width), F32)] * cuts
        + [gate, gate, keep]
        + [send] * groups
        + [pltpu.VMEM((width, columns), BF16)] * (3 * cuts)
        + [pltpu.VMEM((w_out.shape[0] - w_out.shape[0] // 4, w_out.shape[1]), BF16)],
        [SMEM] * 3 + [VMEM] * (cuts + 3) + [HBM] * 4,
        [VMEM] * (4 * cuts + 4 + groups),
        [pltpu.SemaphoreType.DMA((3 * cuts + 1,))],
        flops=12 * rows * width * cuts * columns,
        moved=6 * width * cuts * columns,
    )(*scalars, *tokens, mine, other, embedding, *in_hbm(*weights, w_out))
    factors, (mine_gate, other_gate, keep), result = result[:cuts], result[cuts:cuts + 3], result[cuts + 3:]
    sends, held, out_held = result[:groups], result[groups:-1], result[-1]
    return factors, mine_gate, other_gate, keep, sends, [held[cut::cuts] for cut in range(cuts)], out_held


def later_kernel(added, groups, wanted, tokens_ref, factors_ref, wq_ref, wk_ref, wv_ref, *refs):
    before, (keep_ref, send_ref) = refs[:added], refs[added:]
    kept = keep_ref.shape[0]
    modulated = modulate(tokens_ref[...], factors_ref[...])
    for place, group in enumerate(wanted):
        for i, weight_ref in enumerate((wq_ref, wk_ref, wv_ref)):
            chunk = weight_ref.shape[1] // groups
            projected = dot(modulated, weight_ref[:, group * chunk:(group + 1) * chunk])
            keep, send = projected[:kept], projected[kept:]
            if before:
                sl = slice((group * 3 + i) * chunk, (group * 3 + i + 1) * chunk)
                keep, send = before[0][:, sl] + keep, before[1][:, sl] + send
            sl = slice((place * 3 + i) * chunk, (place * 3 + i + 1) * chunk)
            keep_ref[:, sl] = keep
            send_ref[:, sl] = send


def project_later(tokens, factors, weights, groups, wanted, before=()):
    columns = 3 * weights[0].shape[1] // groups * len(wanted)
    out = pltpu.VMEM((tokens.shape[0], columns), F32)
    return call(
        functools.partial(later_kernel, len(before), groups, wanted),
        [out, out],
        [VMEM] * (5 + len(before)),
        [VMEM] * 2,
        flops=4 * tokens.size * columns,
        moved=2 * tokens.shape[1] * columns,
    )(tokens, *in_vmem(factors, *weights, *before))


def attention_kernel(starts, *refs):
    refs, out_ref = refs[:-1], refs[-1]
    blocks = [(refs[2 * i], refs[2 * i + 1], start) for i, start in enumerate(starts)]
    columns = out_ref.shape[1]

    def part(which, head):
        pieces = []
        for mine, other, start in blocks:
            here = which * columns + head * HD
            there = here + start
            pieces.append((mine[:, there:there + HD] + other[:, here:here + HD]).astype(BF16))
        return jnp.concatenate(pieces, axis=0)

    heads = columns // HD
    all_scores = [
        lax.dot_general(
            part(0, head), part(1, head), (((1,), (1,)), ((), ())), preferred_element_type=F32
        )
        for head in range(heads)
    ]
    all_probs = []
    for scores in all_scores:
        scores = scores * (1.0 / math.sqrt(HD))
        scores = jnp.exp(scores - jnp.max(scores, axis=1, keepdims=True))
        all_probs.append((scores / jnp.sum(scores, axis=1, keepdims=True)).astype(BF16))
    for head, probs in enumerate(all_probs):
        out_ref[:, head * HD:(head + 1) * HD] = dot(probs, part(2, head)).astype(BF16)


def attention(blocks, columns):
    flat = [array for block in blocks for array in block[:2]]
    rows = flat[0].shape[0]
    return call(
        functools.partial(attention_kernel, [block[2] for block in blocks]),
        pltpu.VMEM((rows * len(blocks), columns), BF16),
        [VMEM] * len(flat),
        VMEM,
        flops=4 * (rows * len(blocks)) ** 2 * columns,
        moved=12 * rows * len(blocks) * columns,
    )(*in_vmem(*flat))


def project_mine_kernel(cuts, *refs):
    attended_refs, (gate_ref, held_ref, source_ref, out_ref, rest_ref, sems) = refs[:cuts], refs[cuts:]
    held_rows, columns = held_ref.shape
    copies = []
    size = rest_ref.shape[0] // sems.shape[0]
    for index in range(sems.shape[0]):
        sl = pl.ds(index * size, size)
        there = pl.ds(held_rows + index * size, size)
        copies.append(pltpu.make_async_copy(source_ref.at[there], rest_ref.at[sl], sems.at[index]))
        copies[-1].start()
    chunk = math.gcd(columns, 512)
    attended = jnp.concatenate([ref[...] for ref in attended_refs], axis=1)
    slices = [slice(start, start + chunk) for start in range(0, columns, chunk)]
    partials = [dot(attended[:, :held_rows], held_ref[:, sl]) for sl in slices]
    for copy in copies:
        copy.wait()
    for partial, sl in zip(partials, slices):
        partial = partial + dot(attended[:, held_rows:], rest_ref[:, sl])
        out_ref[:, sl] = gate_ref[:, sl] * partial.astype(BF16).astype(F32)


def project_mine(attended, held, w_out, gate):
    lat, columns = attended[0].shape[0], w_out.shape[1]
    rest = w_out.shape[0] - held.shape[0]
    return call(
        functools.partial(project_mine_kernel, len(attended)),
        [pltpu.VMEM((lat, columns), F32), pltpu.VMEM((rest, columns), BF16)],
        [VMEM] * (2 + len(attended)) + [HBM],
        [VMEM] * 2,
        [pltpu.SemaphoreType.DMA((2,))],
        flops=2 * lat * w_out.size,
        moved=2 * w_out.size,
    )(*attended, *in_vmem(gate, held), *in_hbm(w_out))


def project_other_kernel(cuts, *refs):
    attended_refs, (held_ref, rest_ref, gate_ref, before_ref, *out_refs) = refs[:cuts], refs[cuts:]
    held_rows = held_ref.shape[0]
    rows, columns = out_refs[0].shape
    chunk = math.gcd(columns, 512)
    attended = jnp.concatenate([ref[...] for ref in attended_refs], axis=1)
    for start in range(0, columns, chunk):
        sl = slice(start, start + chunk)
        partial = dot(attended[:, :held_rows], held_ref[:, sl]) + dot(attended[:, held_rows:], rest_ref[:, sl])
        increment = before_ref[:, sl] + gate_ref[:, sl] * partial.astype(BF16).astype(F32)
        for block, out_ref in enumerate(out_refs):
            out_ref[:, sl] = increment[block * rows:(block + 1) * rows]


def project_other(attended, held, rest, gate, before, blocks):
    lat, columns = before.shape
    return call(
        functools.partial(project_other_kernel, len(attended)),
        [pltpu.VMEM((lat // blocks, columns), F32)] * blocks,
        [VMEM] * (4 + len(attended)),
        [VMEM] * blocks,
        flops=4 * lat * held.size,
        moved=4 * held.size,
    )(*attended, *in_vmem(held, rest, gate, before))


def scan_general(parts):
    total = parts[0]
    for mask in range(1, len(parts)):
        total = total + xor_permute(parts[mask].astype(BF16), "tok", mask).astype(F32)
    position = lax.axis_index("tm")
    result, group = total, total
    mask = 1
    while mask < lax.axis_size("tm"):
        received = xor_permute(group.astype(BF16), "tm", mask).astype(F32)
        result = result + jnp.where(position & mask != 0, received, 0.0)
        group = group + received
        mask *= 2
    return result


def scan_planes(parts):
    axes = ("tm", "tok")
    position = lax.axis_index("tm")
    odd = position & 1 == 1
    rows = parts[0].shape[0] // 2

    def near(x):
        return jnp.where(odd, x[rows:], x[:rows])

    def far(x):
        return jnp.where(odd, x[:rows], x[rows:])

    diagonal = xor_permute(far(parts[1]).astype(BF16), axes, 3)
    across = xor_permute(near(parts[1]).astype(BF16), axes, 1)
    beside = xor_permute(far(parts[0]).astype(BF16), axes, 2)
    own_time = near(parts[0]) + across.astype(F32)
    pair_time = beside.astype(F32) + diagonal.astype(F32)
    group = own_time + pair_time
    earlier = jnp.zeros_like(group)
    mask = 2
    while mask < lax.axis_size("tm"):
        received = xor_permute(group.astype(BF16), "tm", mask).astype(F32)
        earlier = earlier + jnp.where(position & mask != 0, received, 0.0)
        group = group + received
        mask *= 2
    own = earlier + own_time + jnp.where(odd, pair_time, 0.0)
    for_pair = earlier + pair_time + jnp.where(odd, 0.0, own_time)
    returned = xor_permute(for_pair.astype(BF16), "tm", 1).astype(F32)
    return jnp.concatenate([jnp.where(odd, returned, own), jnp.where(odd, own, returned)], axis=0)


def body(
    states, start_state, timesteps, guidance_index, modulation, w_query, w_key, w_value, w_out
):
    tok_count = lax.axis_size("tok")
    branch_index = lax.axis_index("branch")
    rows, model_width = states.shape[1:]
    half_width = model_width // 2
    cuts = 2
    normed = normed_half(states[0], branch_index, cuts)
    modulation = into_vmem(jnp.transpose(modulation, (1, 0, 2)), normed[0])
    tokens = [
        [xor_permute(piece, "tok", mask) for piece in normed] for mask in range(1, tok_count)
    ]
    other_modulation = xor_permute(modulation, "branch", 1)
    embedding = embed_half(timesteps, half_width, branch_index)

    columns = w_query.shape[1]
    groups = 2 if columns % (2 * HD) == 0 else 1
    factors, mine_gate, other_gate, keep, sends, weights, out_held = project_first(
        (branch_index[None], timesteps, guidance_index),
        normed, modulation, other_modulation, embedding, (w_query, w_key, w_value), w_out, groups
    )
    blocks = [
        [(keep, xor_permute(send, "branch", 1), 3 * columns // groups * group)]
        for group, send in enumerate(sends)
    ]
    for block in tokens:
        before = ()
        for cut in range(cuts - 1):
            before = project_later(block[cut], factors[cut], weights[cut], groups, range(groups), before)
        for group in range(groups):
            keep, send = project_later(block[-1], factors[-1], weights[-1], groups, [group], before)
            blocks[group].append((keep, xor_permute(send, "branch", 1), 0))
    attended = [attention(blocks[group], columns // groups) for group in range(groups)]
    attended_other = [xor_permute(array, "branch", 1) for array in attended]
    increments, out_rest = project_mine(attended, out_held, w_out, mine_gate)
    parts = project_other(attended_other, out_held, out_rest, other_gate, increments, tok_count)
    pairs = tok_count == 2 and lax.axis_size("tm") % 2 == 0 and rows % 32 == 0
    scan = scan_planes if pairs else scan_general
    return (start_state + scan(parts))[None]


def solution(mesh):
    in_specs = (
        P("tm", "tok", None),
        P("tok", "branch"),
        P("tm"),
        P(),
        P("branch", None, None),
        P("branch", "tok"),
        P("branch", "tok"),
        P("branch", "tok"),
        P("tok", "branch"),
    )
    out_specs = P("tm", "tok", "branch")
    return jax.shard_map(body, mesh=mesh, in_specs=in_specs, out_specs=out_specs, check_vma=False)
```

```python
import functools
import math

import jax
import jax.numpy as jnp
from jax import lax
from jax.experimental import pallas as pl
from jax.experimental.pallas import tpu as pltpu
from jax.sharding import PartitionSpec as P

HD = 128
NSTEPS = 50
F32 = jnp.float32
BF16 = jnp.bfloat16
VMEM = pl.BlockSpec(memory_space=pltpu.VMEM)
SMEM = pl.BlockSpec(memory_space=pltpu.SMEM)
HBM = pl.BlockSpec(memory_space=pltpu.HBM)


def xor_permute(x, axes, mask):
    return lax.ppermute(x, axes, [(i, i ^ mask) for i in range(lax.axis_size(axes))])


def dot(a, b):
    return jnp.dot(a, b, preferred_element_type=F32)


def embed_half(step_ids, half_width, branch_index):
    frequency = jnp.exp(-math.log(10000.0) * jnp.arange(half_width, dtype=F32) / half_width)
    phases = step_ids.astype(F32)[:, None] * frequency[None, :]
    return jnp.where(branch_index == 0, jnp.sin(phases), jnp.cos(phases))


def in_vmem(*arrays):
    return [pltpu.with_memory_space_constraint(array, pltpu.VMEM) for array in arrays]


def in_hbm(*arrays):
    return [pltpu.with_memory_space_constraint(array, pltpu.HBM) for array in arrays]


def call(kernel, out_shape, in_specs, out_specs, scratch_shapes=(), flops=0, moved=0):
    return pl.pallas_call(
        kernel,
        out_shape=out_shape,
        in_specs=in_specs,
        out_specs=out_specs,
        scratch_shapes=scratch_shapes,
        cost_estimate=pl.CostEstimate(flops=flops, bytes_accessed=moved, transcendentals=0),
        compiler_params=pltpu.CompilerParams(vmem_limit_bytes=6 << 20),
    )


def norm_kernel(pieces, branch_ref, states_ref, modulation_ref, held_ref, *refs):
    out_refs, (tokens_ref, sems) = refs[:-2], refs[-2:]
    width = out_refs[0].shape[1]
    rows, model_width = tokens_ref.shape
    size = rows // pieces
    copies = []
    for piece in range(pieces):
        sl = slice(piece * size, (piece + 1) * size)
        copy = pltpu.make_async_copy(states_ref.at[sl], tokens_ref.at[sl], sems.at[piece])
        copy.start()
        copies.append(copy)
    held = pltpu.make_async_copy(modulation_ref, held_ref, sems.at[pieces])
    held.start()
    for piece in range(pieces):
        sl = slice(piece * size, (piece + 1) * size)
        copies[piece].wait()
        tokens = tokens_ref[sl, :]
        mean = jnp.sum(tokens, axis=1, keepdims=True) * (1.0 / model_width)
        centered = tokens - mean
        variance = jnp.sum(centered * centered, axis=1, keepdims=True) * (1.0 / model_width)
        inverse = 1.0 / jnp.sqrt(variance + 1e-06)
        for index, out_ref in enumerate(out_refs):
            start = branch_ref[0] * (model_width // 2) + index * width
            columns = pl.ds(pl.multiple_of(start, HD), width)
            out_ref[sl, :] = (tokens_ref[sl, columns] - mean) * inverse
    held.wait()


def normed_half(states, modulation, branch_index, cuts):
    rows, width = states.shape
    pieces = 1
    return call(
        functools.partial(norm_kernel, pieces),
        [pltpu.VMEM(modulation.shape, F32)] + [pltpu.VMEM((rows, width // 2 // cuts), F32)] * cuts,
        [SMEM, HBM, HBM],
        [VMEM] * (1 + cuts),
        [pltpu.VMEM((rows, width), F32), pltpu.SemaphoreType.DMA((pieces + 1,))],
        moved=4 * rows * width,
    )(branch_index[None], *in_hbm(states, modulation))


def modulate(tokens, factors):
    return jnp.concatenate(
        [
            (tokens * factors[i:i + 1] + factors[i + 1:i + 2]).astype(BF16)
            for i in (0, 2)
        ],
        axis=0,
    )


def first_kernel(cuts, groups, branch_ref, *refs):
    tokens_refs, refs = refs[:cuts], refs[cuts:]
    mine_ref, other_ref, embedding_ref, *sources, out_source = refs[:7]
    factor_refs, refs = refs[7:7 + cuts], refs[7 + cuts:]
    keep_ref, refs = refs[0], refs[1:]
    send_refs, targets, (out_target, sems) = refs[:groups], refs[groups:-2], refs[-2:]
    width = tokens_refs[0].shape[1]
    copies = []
    for i, source in enumerate(sources):
        for cut in range(cuts):
            copies.append(
                pltpu.make_async_copy(
                    source.at[pl.ds(cut * width, width)], targets[i * cuts + cut], sems.at[i * cuts + cut]
                )
            )
    held_rows = out_source.at[pl.ds(0, out_target.shape[0])]
    copies.append(pltpu.make_async_copy(held_rows, out_target, sems.at[len(copies)]))
    for copy in copies:
        copy.start()

    base = branch_ref[0] * (width * cuts)
    modulated = []
    for cut in range(cuts):
        columns = pl.ds(pl.multiple_of(base + cut * width, HD), width)
        embedding = embedding_ref[:, cut * width:(cut + 1) * width]
        rows = []
        for mod_ref in (mine_ref, other_ref):
            rows += [1.0 + mod_ref[1, :, columns], mod_ref[0, :, columns] + embedding]
        for i, row in enumerate(rows):
            factor_refs[cut][i:i + 1, :] = row
        modulated.append(modulate(tokens_refs[cut][...], rows_of(rows)))
    kept = keep_ref.shape[0]
    for i in range(len(sources)):
        chunk = sources[i].shape[1] // groups
        for cut in range(cuts):
            copies[i * cuts + cut].wait()
        for group in range(groups):
            columns = slice(group * chunk, (group + 1) * chunk)
            projected = sum(
                dot(modulated[cut], targets[i * cuts + cut][:, columns]) for cut in range(cuts)
            )
            here = (group * 3 + i) * chunk
            keep_ref[:, here:here + chunk] = projected[:kept]
            send_refs[group][:, i * chunk:(i + 1) * chunk] = projected[kept:]
    copies[-1].wait()


def rows_of(rows):
    return jnp.concatenate(rows, axis=0)


def project_first(branch_index, tokens, mine, other, embedding, weights, w_out, groups):
    cuts = len(tokens)
    rows, width = tokens[0].shape
    columns = weights[0].shape[1]
    keep = pltpu.VMEM((rows, 3 * columns), F32)
    send = pltpu.VMEM((rows, 3 * columns // groups), F32)
    result = call(
        functools.partial(first_kernel, cuts, groups),
        [pltpu.VMEM((4, width), F32)] * cuts
        + [keep]
        + [send] * groups
        + [pltpu.VMEM((width, columns), BF16)] * (3 * cuts)
        + [pltpu.VMEM((w_out.shape[0] - w_out.shape[0] // 4, w_out.shape[1]), BF16)],
        [SMEM] + [VMEM] * (cuts + 3) + [HBM] * 4,
        [VMEM] * (4 * cuts + 2 + groups),
        [pltpu.SemaphoreType.DMA((3 * cuts + 1,))],
        flops=12 * rows * width * cuts * columns,
        moved=6 * width * cuts * columns,
    )(branch_index[None], *tokens, mine, other, embedding, *in_hbm(*weights, w_out))
    factors, keep, result = result[:cuts], result[cuts], result[cuts + 1:]
    sends, held, out_held = result[:groups], result[groups:-1], result[-1]
    return factors, keep, sends, [held[cut::cuts] for cut in range(cuts)], out_held


def later_kernel(added, groups, wanted, tokens_ref, factors_ref, wq_ref, wk_ref, wv_ref, *refs):
    before, (keep_ref, send_ref) = refs[:added], refs[added:]
    kept = keep_ref.shape[0]
    modulated = modulate(tokens_ref[...], factors_ref[...])
    for place, group in enumerate(wanted):
        for i, weight_ref in enumerate((wq_ref, wk_ref, wv_ref)):
            chunk = weight_ref.shape[1] // groups
            projected = dot(modulated, weight_ref[:, group * chunk:(group + 1) * chunk])
            keep, send = projected[:kept], projected[kept:]
            if before:
                sl = slice((group * 3 + i) * chunk, (group * 3 + i + 1) * chunk)
                keep, send = before[0][:, sl] + keep, before[1][:, sl] + send
            sl = slice((place * 3 + i) * chunk, (place * 3 + i + 1) * chunk)
            keep_ref[:, sl] = keep
            send_ref[:, sl] = send


def project_later(tokens, factors, weights, groups, wanted, before=()):
    columns = 3 * weights[0].shape[1] // groups * len(wanted)
    out = pltpu.VMEM((tokens.shape[0], columns), F32)
    return call(
        functools.partial(later_kernel, len(before), groups, wanted),
        [out, out],
        [VMEM] * (5 + len(before)),
        [VMEM] * 2,
        flops=4 * tokens.size * columns,
        moved=2 * tokens.shape[1] * columns,
    )(tokens, *in_vmem(factors, *weights, *before))


def attention_kernel(starts, *refs):
    refs, out_ref = refs[:-1], refs[-1]
    blocks = [(refs[2 * i], refs[2 * i + 1], start) for i, start in enumerate(starts)]
    columns = out_ref.shape[1]

    def part(which, head):
        pieces = []
        for mine, other, start in blocks:
            here = which * columns + head * HD
            there = here + start
            pieces.append((mine[:, there:there + HD] + other[:, here:here + HD]).astype(BF16))
        return jnp.concatenate(pieces, axis=0)

    heads = columns // HD
    all_scores = [
        lax.dot_general(
            part(0, head), part(1, head), (((1,), (1,)), ((), ())), preferred_element_type=F32
        )
        for head in range(heads)
    ]
    all_probs = []
    for scores in all_scores:
        scores = scores * (1.0 / math.sqrt(HD))
        scores = jnp.exp(scores - jnp.max(scores, axis=1, keepdims=True))
        all_probs.append((scores / jnp.sum(scores, axis=1, keepdims=True)).astype(BF16))
    for head, probs in enumerate(all_probs):
        out_ref[:, head * HD:(head + 1) * HD] = dot(probs, part(2, head)).astype(BF16)


def attention(blocks, columns):
    flat = [array for block in blocks for array in block[:2]]
    rows = flat[0].shape[0]
    return call(
        functools.partial(attention_kernel, [block[2] for block in blocks]),
        pltpu.VMEM((rows * len(blocks), columns), BF16),
        [VMEM] * len(flat),
        VMEM,
        flops=4 * (rows * len(blocks)) ** 2 * columns,
        moved=12 * rows * len(blocks) * columns,
    )(*in_vmem(*flat))


def gate_of(mine, branch_ref, step_ref, guidance_ref, modulation_ref, columns):
    step = 2.0 * (1.0 + step_ref[0].astype(F32)) / NSTEPS
    scale = 1.5 + 0.5 * guidance_ref[0].astype(F32)
    conditional = (branch_ref[0] == 0) == mine
    share = jnp.where(conditional, step * scale, step * (1.0 - scale))
    half = pl.ds(pl.multiple_of(branch_ref[0] * columns, HD), columns)
    return share * (1.0 + modulation_ref[2, :, half])


def project_mine_kernel(cuts, *refs):
    scalar_refs, attended_refs, refs = refs[:3], refs[3:3 + cuts], refs[3 + cuts:]
    modulation_ref, held_ref, source_ref, out_ref, rest_ref, sems = refs
    held_rows, columns = held_ref.shape
    copies = []
    size = rest_ref.shape[0] // sems.shape[0]
    for index in range(sems.shape[0]):
        sl = pl.ds(index * size, size)
        there = pl.ds(held_rows + index * size, size)
        copies.append(pltpu.make_async_copy(source_ref.at[there], rest_ref.at[sl], sems.at[index]))
        copies[-1].start()
    chunk = math.gcd(columns, 512)
    attended = jnp.concatenate([ref[...] for ref in attended_refs], axis=1)
    slices = [slice(start, start + chunk) for start in range(0, columns, chunk)]
    partials = [dot(attended[:, :held_rows], held_ref[:, sl]) for sl in slices]
    gate = gate_of(True, *scalar_refs, modulation_ref, columns)
    for copy in copies:
        copy.wait()
    for partial, sl in zip(partials, slices):
        partial = partial + dot(attended[:, held_rows:], rest_ref[:, sl])
        out_ref[:, sl] = gate[:, sl] * partial.astype(BF16).astype(F32)


def project_mine(scalars, attended, held, w_out, modulation):
    lat, columns = attended[0].shape[0], w_out.shape[1]
    rest = w_out.shape[0] - held.shape[0]
    return call(
        functools.partial(project_mine_kernel, len(attended)),
        [pltpu.VMEM((lat, columns), F32), pltpu.VMEM((rest, columns), BF16)],
        [SMEM] * 3 + [VMEM] * (2 + len(attended)) + [HBM],
        [VMEM] * 2,
        [pltpu.SemaphoreType.DMA((2,))],
        flops=2 * lat * w_out.size,
        moved=2 * w_out.size,
    )(*scalars, *attended, modulation, *in_vmem(held), *in_hbm(w_out))


def project_other_kernel(cuts, *refs):
    scalar_refs, attended_refs, refs = refs[:3], refs[3:3 + cuts], refs[3 + cuts:]
    modulation_ref, held_ref, rest_ref, before_ref, *out_refs = refs
    held_rows = held_ref.shape[0]
    rows, columns = out_refs[0].shape
    chunk = math.gcd(columns, 512)
    gate = gate_of(False, *scalar_refs, modulation_ref, columns)
    attended = jnp.concatenate([ref[...] for ref in attended_refs], axis=1)
    for start in range(0, columns, chunk):
        sl = slice(start, start + chunk)
        partial = dot(attended[:, :held_rows], held_ref[:, sl]) + dot(attended[:, held_rows:], rest_ref[:, sl])
        increment = before_ref[:, sl] + gate[:, sl] * partial.astype(BF16).astype(F32)
        for block, out_ref in enumerate(out_refs):
            out_ref[:, sl] = increment[block * rows:(block + 1) * rows]


def project_other(scalars, attended, held, rest, modulation, before, blocks):
    lat, columns = before.shape
    return call(
        functools.partial(project_other_kernel, len(attended)),
        [pltpu.VMEM((lat // blocks, columns), F32)] * blocks,
        [SMEM] * 3 + [VMEM] * (4 + len(attended)),
        [VMEM] * blocks,
        flops=4 * lat * held.size,
        moved=4 * held.size,
    )(*scalars, *attended, modulation, *in_vmem(held, rest, before))


def scan_general(parts):
    total = parts[0]
    for mask in range(1, len(parts)):
        total = total + xor_permute(parts[mask].astype(BF16), "tok", mask).astype(F32)
    position = lax.axis_index("tm")
    result, group = total, total
    mask = 1
    while mask < lax.axis_size("tm"):
        received = xor_permute(group.astype(BF16), "tm", mask).astype(F32)
        result = result + jnp.where(position & mask != 0, received, 0.0)
        group = group + received
        mask *= 2
    return result


def scan_planes(parts):
    axes = ("tm", "tok")
    position = lax.axis_index("tm")
    odd = position & 1 == 1
    rows = parts[0].shape[0] // 2

    def near(x):
        return jnp.where(odd, x[rows:], x[:rows])

    def far(x):
        return jnp.where(odd, x[:rows], x[rows:])

    diagonal = xor_permute(far(parts[1]).astype(BF16), axes, 3)
    across = xor_permute(near(parts[1]).astype(BF16), axes, 1)
    beside = xor_permute(far(parts[0]).astype(BF16), axes, 2)
    own_time = near(parts[0]) + across.astype(F32)
    pair_time = beside.astype(F32) + diagonal.astype(F32)
    group = own_time + pair_time
    earlier = jnp.zeros_like(group)
    mask = 2
    while mask < lax.axis_size("tm"):
        received = xor_permute(group.astype(BF16), "tm", mask).astype(F32)
        earlier = earlier + jnp.where(position & mask != 0, received, 0.0)
        group = group + received
        mask *= 2
    own = earlier + own_time + jnp.where(odd, pair_time, 0.0)
    for_pair = earlier + pair_time + jnp.where(odd, 0.0, own_time)
    returned = xor_permute(for_pair.astype(BF16), "tm", 1).astype(F32)
    return jnp.concatenate([jnp.where(odd, returned, own), jnp.where(odd, own, returned)], axis=0)


def body(
    states, start_state, timesteps, guidance_index, modulation, w_query, w_key, w_value, w_out
):
    tok_count = lax.axis_size("tok")
    branch_index = lax.axis_index("branch")
    rows, model_width = states.shape[1:]
    half_width = model_width // 2
    cuts = 1
    modulation, *normed = normed_half(
        states[0], jnp.transpose(modulation, (1, 0, 2)), branch_index, cuts
    )
    tokens = [
        [xor_permute(piece.astype(jnp.float16), "tok", mask).astype(F32) for piece in normed]
        for mask in range(1, tok_count)
    ]
    other_modulation = xor_permute(modulation, "branch", 1)
    embedding = embed_half(timesteps, half_width, branch_index)

    columns = w_query.shape[1]
    groups = 2 if columns % (2 * HD) == 0 else 1
    factors, keep, sends, weights, out_held = project_first(
        branch_index, normed, modulation, other_modulation, embedding,
        (w_query, w_key, w_value), w_out, groups
    )
    blocks = [
        [(keep, xor_permute(send, "branch", 1), 3 * columns // groups * group)]
        for group, send in enumerate(sends)
    ]
    for block in tokens:
        before = ()
        for cut in range(cuts - 1):
            before = project_later(block[cut], factors[cut], weights[cut], groups, range(groups), before)
        for group in range(groups):
            keep, send = project_later(block[-1], factors[-1], weights[-1], groups, [group], before)
            blocks[group].append((keep, xor_permute(send, "branch", 1), 0))
    attended = [attention(blocks[group], columns // groups) for group in range(groups)]
    attended_other = [xor_permute(array, "branch", 1) for array in attended]
    scalars = (branch_index[None], timesteps, guidance_index)
    increments, out_rest = project_mine(scalars, attended, out_held, w_out, modulation)
    parts = project_other(
        scalars, attended_other, out_held, out_rest, other_modulation, increments, tok_count
    )
    pairs = tok_count == 2 and lax.axis_size("tm") % 2 == 0 and rows % 32 == 0
    scan = scan_planes if pairs else scan_general
    return (start_state + scan(parts))[None]


def solution(mesh):
    in_specs = (
        P("tm", "tok", None),
        P("tok", "branch"),
        P("tm"),
        P(),
        P("branch", None, None),
        P("branch", "tok"),
        P("branch", "tok"),
        P("branch", "tok"),
        P("tok", "branch"),
    )
    out_specs = P("tm", "tok", "branch")
    return jax.shard_map(body, mesh=mesh, in_specs=in_specs, out_specs=out_specs, check_vma=False)
```

```python
import functools
import math

import jax
import jax.numpy as jnp
from jax import lax
from jax.experimental import pallas as pl
from jax.experimental.pallas import tpu as pltpu
from jax.sharding import PartitionSpec as P

HD = 128
NSTEPS = 50
F32 = jnp.float32
BF16 = jnp.bfloat16
VMEM = pl.BlockSpec(memory_space=pltpu.VMEM)
SMEM = pl.BlockSpec(memory_space=pltpu.SMEM)
ANY = pl.BlockSpec(memory_space=pl.ANY)
HBM = pl.BlockSpec(memory_space=pltpu.HBM)


def xor_permute(x, axes, mask):
    return lax.ppermute(x, axes, [(i, i ^ mask) for i in range(lax.axis_size(axes))])


def dot(a, b):
    return jnp.dot(a, b, preferred_element_type=F32)


def embed_half(step_ids, half_width, branch_index):
    frequency = jnp.exp(-math.log(10000.0) * jnp.arange(half_width, dtype=F32) / half_width)
    phases = step_ids.astype(F32)[:, None] * frequency[None, :]
    return jnp.where(branch_index == 0, jnp.sin(phases), jnp.cos(phases))


def in_vmem(*arrays):
    return [pltpu.with_memory_space_constraint(array, pltpu.VMEM) for array in arrays]


def in_hbm(*arrays):
    return [pltpu.with_memory_space_constraint(array, pltpu.HBM) for array in arrays]


def call(kernel, out_shape, in_specs, out_specs, scratch_shapes=(), aliases=None, flops=0, moved=0):
    return pl.pallas_call(
        kernel,
        out_shape=out_shape,
        in_specs=in_specs,
        out_specs=out_specs,
        scratch_shapes=scratch_shapes,
        input_output_aliases=aliases or {},
        cost_estimate=pl.CostEstimate(flops=flops, bytes_accessed=moved, transcendentals=0),
        compiler_params=pltpu.CompilerParams(vmem_limit_bytes=6 << 20),
    )


def norm_kernel(branch_ref, states_ref, modulation_ref, held_ref, *refs):
    out_refs, (tokens_ref, sems) = refs[:-2], refs[-2:]
    rows, model_width = tokens_ref.shape
    pieces = sems.shape[0] - 1
    size = rows // pieces
    copies = []
    for piece in range(pieces):
        sl = pl.ds(piece * size, size)
        copies.append(pltpu.make_async_copy(states_ref.at[sl], tokens_ref.at[sl], sems.at[piece]))
    copies.append(pltpu.make_async_copy(modulation_ref, held_ref, sems.at[pieces]))
    for copy in copies:
        copy.start()
    for copy in copies:
        copy.wait()
    tokens = tokens_ref[...]
    mean = jnp.sum(tokens, axis=1, keepdims=True) * (1.0 / model_width)
    centered = tokens - mean
    variance = jnp.sum(centered * centered, axis=1, keepdims=True) * (1.0 / model_width)
    inverse = 1.0 / jnp.sqrt(variance + 1e-06)
    start = branch_ref[0] * (model_width // 2)
    for out_ref in out_refs:
        width = out_ref.shape[1]
        columns = pl.ds(pl.multiple_of(start, HD), width)
        out_ref[...] = (tokens_ref[:, columns] - mean) * inverse
        start = start + width


def normed_half(states, modulation, branch_index, widths):
    rows, width = states.shape
    pieces = 1
    return call(
        norm_kernel,
        [pltpu.VMEM(modulation.shape, F32)] + [pltpu.VMEM((rows, size), F32) for size in widths],
        [SMEM, HBM, HBM],
        [VMEM] * (1 + len(widths)),
        [pltpu.VMEM((rows, width), F32), pltpu.SemaphoreType.DMA((pieces + 1,))],
        moved=4 * rows * width,
    )(branch_index[None], *in_hbm(states, modulation))


def same_kernel(array_ref, _, out_ref):
    pass


def same(array, after):
    return call(
        same_kernel, pltpu.VMEM(array.shape, array.dtype), [VMEM, ANY], VMEM, aliases={0: 0}
    )(*in_vmem(array), after)


def modulate(tokens, factors):
    return jnp.concatenate(
        [
            (tokens * factors[i:i + 1] + factors[i + 1:i + 2] + factors[4:5]).astype(BF16)
            for i in (0, 2)
        ],
        axis=0,
    )


def first_kernel(groups, cuts, branch_ref, *refs):
    tokens_refs, refs = refs[:cuts], refs[cuts:]
    mine_ref, other_ref, embedding_ref, *sources = refs[:7]
    factors_refs, (keep_ref, *refs) = refs[7:7 + cuts], refs[7 + cuts:]
    send_refs, targets, sems = refs[:groups], refs[groups:-1], refs[-1]
    kept = keep_ref.shape[0]
    width = embedding_ref.shape[1]
    pieces = sems.shape[0] // len(sources)
    copies = []
    for source, target in zip(sources, targets):
        size = target.shape[0] // pieces
        for piece in range(pieces):
            sl = pl.ds(piece * size, size)
            copies.append(pltpu.make_async_copy(source.at[sl], target.at[sl], sems.at[len(copies)]))
    for copy in copies:
        copy.start()

    start = 0
    modulated = []
    for tokens_ref, factors_ref in zip(tokens_refs, factors_refs):
        size = tokens_ref.shape[1]
        columns = pl.ds(pl.multiple_of(branch_ref[0] * width + start, HD), size)
        embedding = embedding_ref[:, start:start + size]
        rows = []
        for mod_ref in (mine_ref, other_ref):
            rows += [1.0 + mod_ref[1, :, columns], mod_ref[0, :, columns]]
        rows.append(embedding)
        for i, row in enumerate(rows):
            factors_ref[i:i + 1, :] = row
        modulated.append(modulate(tokens_ref[...], rows_of(rows)))
        start += size
    modulated = jnp.concatenate(modulated, axis=1)
    size = width // pieces
    for i, weight_ref in enumerate(targets[:3]):
        projected = None
        for piece in range(pieces):
            copies[i * pieces + piece].wait()
            sl = slice(piece * size, (piece + 1) * size)
            partial = dot(modulated[:, sl], weight_ref[sl, :])
            projected = partial if projected is None else projected + partial
        chunk = weight_ref.shape[1] // groups
        for group in range(groups):
            columns = slice(group * chunk, (group + 1) * chunk)
            here = (group * 3 + i) * chunk
            keep_ref[:, here:here + chunk] = projected[:kept, columns]
            send_refs[group][:, i * chunk:(i + 1) * chunk] = projected[kept:, columns]
    for copy in copies[3 * pieces:]:
        copy.wait()


def rows_of(rows):
    return jnp.concatenate(rows, axis=0)


def project_first(branch_index, tokens, mine, other, embedding, weights, w_out, groups):
    rows = tokens[0].shape[0]
    width, columns = weights[0].shape
    cuts = len(tokens)
    factors = [pltpu.VMEM((5, piece.shape[1]), F32) for piece in tokens]
    keep = pltpu.VMEM((rows, 3 * columns), F32)
    send = pltpu.VMEM((rows, 3 * columns // groups), F32)
    held = [pltpu.VMEM(w.shape, BF16) for w in weights]
    out_held = pltpu.VMEM((w_out.shape[0] - w_out.shape[0] // 4, w_out.shape[1]), BF16)
    result = call(
        functools.partial(first_kernel, groups, cuts),
        factors + [keep] + [send] * groups + held + [out_held],
        [SMEM] + [VMEM] * (3 + cuts) + [HBM] * 4,
        [VMEM] * (5 + cuts + groups),
        [pltpu.SemaphoreType.DMA((12,))],
        flops=12 * rows * width * columns,
        moved=6 * width * columns,
    )(branch_index[None], *tokens, mine, other, embedding, *in_hbm(*weights, w_out))
    factors, (keep, *result) = result[:cuts], result[cuts:]
    return factors, keep, result[:groups], result[groups:-1], result[-1]


def later_kernel(added, groups, wanted, first_row, tokens_ref, factors_ref, wq_ref, wk_ref, wv_ref, *refs):
    before, (keep_ref, send_ref) = refs[:added], refs[-2:]
    rows = slice(first_row, first_row + tokens_ref.shape[1])
    kept = keep_ref.shape[0]
    modulated = modulate(tokens_ref[...], factors_ref[...])
    for place, group in enumerate(wanted):
        for i, weight_ref in enumerate((wq_ref, wk_ref, wv_ref)):
            chunk = weight_ref.shape[1] // groups
            projected = dot(modulated, weight_ref[rows, group * chunk:(group + 1) * chunk])
            keep, send = projected[:kept], projected[kept:]
            if before:
                sl = slice((group * 3 + i) * chunk, (group * 3 + i + 1) * chunk)
                keep, send = before[0][:, sl] + keep, before[1][:, sl] + send
            sl = slice((place * 3 + i) * chunk, (place * 3 + i + 1) * chunk)
            keep_ref[:, sl] = keep
            send_ref[:, sl] = send


def project_later(tokens, factors, weights, groups, wanted, first_row, before=(), scalars=()):
    columns = 3 * weights[0].shape[1] // groups * len(wanted)
    out = pltpu.VMEM((tokens.shape[0], columns), F32)
    return call(
        functools.partial(later_kernel, len(before), groups, wanted, first_row),
        [out, out],
        [VMEM] * (5 + len(before)) + [SMEM] * len(scalars),
        [VMEM] * 2,
        flops=4 * tokens.size * columns,
        moved=2 * tokens.shape[1] * columns,
    )(tokens, *in_vmem(factors, *weights, *before), *scalars)


def attention_kernel(starts, *refs):
    refs, out_ref = refs[:-1], refs[-1]
    blocks = [(refs[2 * i], refs[2 * i + 1], start) for i, start in enumerate(starts)]
    columns = out_ref.shape[1]

    def part(which, head):
        pieces = []
        for mine, other, start in blocks:
            here = which * columns + head * HD
            there = here + start
            pieces.append((mine[:, there:there + HD] + other[:, here:here + HD]).astype(BF16))
        return jnp.concatenate(pieces, axis=0)

    heads = columns // HD
    all_scores = [
        lax.dot_general(
            part(0, head), part(1, head), (((1,), (1,)), ((), ())), preferred_element_type=F32
        )
        for head in range(heads)
    ]
    all_probs = []
    for scores in all_scores:
        scores = scores * (1.0 / math.sqrt(HD))
        scores = jnp.exp(scores - jnp.max(scores, axis=1, keepdims=True))
        all_probs.append((scores / jnp.sum(scores, axis=1, keepdims=True)).astype(BF16))
    for head, probs in enumerate(all_probs):
        out_ref[:, head * HD:(head + 1) * HD] = dot(probs, part(2, head)).astype(BF16)


def attention(blocks, columns):
    flat = [array for block in blocks for array in block[:2]]
    rows = flat[0].shape[0]
    return call(
        functools.partial(attention_kernel, [block[2] for block in blocks]),
        pltpu.VMEM((rows * len(blocks), columns), BF16),
        [VMEM] * len(flat),
        VMEM,
        flops=4 * (rows * len(blocks)) ** 2 * columns,
        moved=12 * rows * len(blocks) * columns,
    )(*in_vmem(*flat))


def gate_of(mine, branch_ref, step_ref, guidance_ref, modulation_ref, columns):
    step = 2.0 * (1.0 + step_ref[0].astype(F32)) / NSTEPS
    scale = 1.5 + 0.5 * guidance_ref[0].astype(F32)
    conditional = (branch_ref[0] == 0) == mine
    share = jnp.where(conditional, step * scale, step * (1.0 - scale))
    half = pl.ds(pl.multiple_of(branch_ref[0] * columns, HD), columns)
    return share * (1.0 + modulation_ref[2, :, half])


def rest_kernel(source_ref, _, out_ref, sems):
    rows = out_ref.shape[0]
    size = rows // sems.shape[0]
    copies = []
    for index in range(sems.shape[0]):
        there = pl.ds(source_ref.shape[0] - rows + index * size, size)
        here = pl.ds(index * size, size)
        copies.append(pltpu.make_async_copy(source_ref.at[there], out_ref.at[here], sems.at[index]))
        copies[-1].start()
    for copy in copies:
        copy.wait()


def last_rows(array, rows, after):
    return call(
        rest_kernel,
        pltpu.VMEM((rows, array.shape[1]), array.dtype),
        [HBM, ANY],
        VMEM,
        [pltpu.SemaphoreType.DMA((1,))],
        moved=2 * rows * array.shape[1],
    )(*in_hbm(array), after)


def project_kernel(mine, cuts, added, *refs):
    scalar_refs, attended_refs, refs = refs[:3], refs[3:3 + cuts], refs[3 + cuts:]
    modulation_ref, held_ref, rest_ref, *refs = refs
    before, out_refs = refs[:added], refs[added:]
    held_rows = held_ref.shape[0]
    rows, columns = out_refs[0].shape
    chunk = math.gcd(columns, 512)
    gate = gate_of(mine, *scalar_refs, modulation_ref, columns)
    attended = jnp.concatenate([ref[...] for ref in attended_refs], axis=1)
    for start in range(0, columns, chunk):
        sl = slice(start, start + chunk)
        partial = dot(attended[:, :held_rows], held_ref[:, sl]) + dot(attended[:, held_rows:], rest_ref[:, sl])
        increment = gate[:, sl] * partial.astype(BF16).astype(F32)
        if before:
            increment = before[0][:, sl] + increment
        for block, out_ref in enumerate(out_refs):
            out_ref[:, sl] = increment[block * rows:(block + 1) * rows]


def project(mine, scalars, attended, held, rest, modulation, before=(), blocks=1):
    lat, columns = attended[0].shape[0], held.shape[1]
    return call(
        functools.partial(project_kernel, mine, len(attended), len(before)),
        [pltpu.VMEM((lat // blocks, columns), F32)] * blocks,
        [SMEM] * 3 + [VMEM] * (3 + len(attended) + len(before)),
        [VMEM] * blocks,
        flops=2 * lat * columns * (held.shape[0] + rest.shape[0]),
        moved=2 * columns * (held.shape[0] + rest.shape[0]),
    )(*scalars, *attended, modulation, *in_vmem(held, rest, *before))


def finish_kernel(place_ref, start_ref, added_ref, *refs):
    refs[-1][...] = start_ref[...] + added_ref[...].astype(F32)


def finish(place, start_state, added, target=None):
    rows, columns = added.shape
    half = pl.BlockSpec((rows, columns), lambda step, place_ref: (place_ref[0], 0))
    whole = pl.BlockSpec((rows, columns), lambda step, place_ref: (0, 0))
    given = [] if target is None else [target]
    return pl.pallas_call(
        finish_kernel,
        out_shape=jax.ShapeDtypeStruct(start_state.shape, F32),
        grid_spec=pltpu.PrefetchScalarGridSpec(
            num_scalar_prefetch=1,
            grid=(1,),
            in_specs=[half, whole] + [ANY] * len(given),
            out_specs=half,
        ),
        input_output_aliases={3: 0} if given else {},
        compiler_params=pltpu.CompilerParams(vmem_limit_bytes=6 << 20),
    )(place[None], start_state, added, *given)


def scan_general(parts, start_state):
    total = parts[0]
    for mask in range(1, len(parts)):
        total = total + xor_permute(parts[mask].astype(BF16), "tok", mask).astype(F32)
    position = lax.axis_index("tm")
    result, group = total, total
    mask = 1
    while mask < lax.axis_size("tm"):
        received = xor_permute(group.astype(BF16), "tm", mask).astype(F32)
        result = result + jnp.where(position & mask != 0, received, 0.0)
        group = group + received
        mask *= 2
    return start_state + result


def scan_planes(parts, start_state):
    axes = ("tm", "tok")
    position = lax.axis_index("tm")
    odd = position & 1 == 1
    rows = parts[0].shape[0] // 2

    def near(x):
        return jnp.where(odd, x[rows:], x[:rows])

    def far(x):
        return jnp.where(odd, x[:rows], x[rows:])

    diagonal = xor_permute(far(parts[1]).astype(BF16), axes, 3)
    across = xor_permute(near(parts[1]).astype(BF16), axes, 1)
    beside = xor_permute(far(parts[0]).astype(BF16), axes, 2)
    own_time = near(parts[0]) + across.astype(F32)
    pair_time = beside.astype(F32) + diagonal.astype(F32)
    group = own_time + pair_time
    earlier = jnp.zeros_like(group)
    mask = 2
    while mask < lax.axis_size("tm"):
        received = xor_permute(group.astype(BF16), "tm", mask).astype(F32)
        earlier = earlier + jnp.where(position & mask != 0, received, 0.0)
        group = group + received
        mask *= 2
    own = earlier + own_time + jnp.where(odd, pair_time, 0.0)
    for_pair = earlier + pair_time + jnp.where(odd, 0.0, own_time)
    returned = xor_permute(for_pair.astype(BF16), "tm", 1)
    place = position & 1
    return finish(1 - place, start_state, returned, finish(place, start_state, own))


def body(
    states, start_state, timesteps, guidance_index, modulation, w_query, w_key, w_value, w_out
):
    tok_count = lax.axis_size("tok")
    branch_index = lax.axis_index("branch")
    rows, model_width = states.shape[1:]
    half_width = model_width // 2
    widths = (half_width // 2, half_width // 2)
    modulation, *normed = normed_half(
        states[0], jnp.transpose(modulation, (1, 0, 2)), branch_index, widths
    )
    tokens = [
        [xor_permute(piece, "tok", mask) for piece in normed]
        for mask in range(1, tok_count)
    ]
    embedding = embed_half(timesteps, half_width, branch_index)
    modulation = same(modulation, embedding)
    other_modulation = xor_permute(modulation, "branch", 1)

    columns = w_query.shape[1]
    groups = 2 if columns % (2 * HD) == 0 else 1
    factors, keep, sends, weights, out_held = project_first(
        branch_index, normed, modulation, other_modulation, embedding,
        (w_query, w_key, w_value), w_out, groups
    )
    blocks = [
        [(keep, xor_permute(send, "branch", 1), 3 * columns // groups * group)]
        for group, send in enumerate(sends)
    ]
    for block in tokens:
        first_row, before = 0, ()
        for piece, factor in zip(block[:-1], factors):
            before = project_later(
                piece, factor, weights, groups, range(groups), first_row, before, (guidance_index,)
            )
            first_row += piece.shape[1]
        for group in range(groups):
            keep, send = project_later(
                block[-1], factors[-1], weights, groups, [group], first_row, before
            )
            blocks[group].append((keep, xor_permute(send, "branch", 1), 0))
    attended = [attention(blocks[group], columns // groups) for group in range(groups)]
    attended_other = [xor_permute(array, "branch", 1) for array in attended]
    scalars = (branch_index[None], timesteps, guidance_index)
    out_rest = last_rows(w_out, w_out.shape[0] - out_held.shape[0], attended[0])
    increments = project(True, scalars, attended, out_held, out_rest, modulation)
    parts = project(
        False, scalars, attended_other, out_held, out_rest, other_modulation, increments, tok_count
    )
    pairs = tok_count == 2 and lax.axis_size("tm") % 2 == 0 and rows % 32 == 0
    scan = scan_planes if pairs else scan_general
    return scan(parts, start_state)[None]


def solution(mesh):
    in_specs = (
        P("tm", "tok", None),
        P("tok", "branch"),
        P("tm"),
        P(),
        P("branch", None, None),
        P("branch", "tok"),
        P("branch", "tok"),
        P("branch", "tok"),
        P("tok", "branch"),
    )
    out_specs = P("tm", "tok", "branch")
    return jax.shard_map(body, mesh=mesh, in_specs=in_specs, out_specs=out_specs, check_vma=False)
```
